32 devices in a mesh: gx: 4 (over y, x), gy: 8 (over z, core).
Axes of the slice: x: 2, y: 2, z: 4, core: 2. Of those that a mesh axis runs over, the one named last changes fastest.
Arguments:
- terminal_elevation: float32 [8, 1024, 1024], P(None, 'gx', 'gy'), may hold values from -6 to 6
- terminal_flux_x: float32 [8, 1024, 1024], P(None, 'gx', 'gy'), may hold values from -6 to 6
- terminal_flux_y: float32 [8, 1024, 1024], P(None, 'gx', 'gy'), may hold values from -6 to 6
- courant_x: float32 [1024, 1024], P('gx', 'gy'), may hold values from 0 to 0.45, as said below
- courant_y: float32 [1024, 1024], P('gx', 'gy'), may hold values from 0 to 0.45, as said below
- land_sea: int32 [1024, 1024], P('gx', 'gy'), may hold values from 0 to 1
- uplift: float32 [1024, 1024], P('gx', 'gy'), may hold values from 0.1 to 1
- tile_patches: int32 [4, 8, 15], replicated, may hold values from 0 to 255, as said below
- patch_home: int32 [256], replicated, may hold values from 0 to 255, each once
Outputs:
- adjoint_elevation: float32 [8, 1024, 1024], P(None, 'gx', 'gy')
- patch_gradient: float32 [256, 8], P(('gx', 'gy'))
The draws below stay inside these ranges and needn't reach their ends.
Inputs may be any that keep to these rules, and one draw needn't show every extreme that they name: tile_patches[a, b, s] for s = u * 3 + w is the patch whose footprint covers the cells of tile a, b at slot s; footprints are squares of 64 cells offset by 32, the last one wrapping to the first, so every patch is listed by one to four tiles consistently. `courant_x`: zero on every face next to a land cell and on the faces past the grid's last row; sums of the two numbers of a cell stay under one. `courant_y`: zero on every face next to a land cell and on the faces past the grid's last column.
All inputs are finite; a program needn't handle non-finite values.
Results may differ from the reference program's by a relative error of at most 0.00026.
Values sent between devices are 32-bit elements; how exact they have to be, the bound alone decides.
No kernel may reach another device: no remote copies, remote signals or barrier semaphores. Data moves between devices by JAX's collectives and lax.ppermute only.
A program may use at most 64 MiB of HBM per device.

```python
import math
import jax
import jax.numpy as jnp
from jax import lax

GAUGES = 8
CX = 256
CY = 128
BS = 64
ITERS = 8
NX = 1024
NY = 1024
TILES_X = 4
TILES_Y = 8
PATCHES = 256


def wet_field(key):
    folded = jax.random.fold_in(key, 7)
    row_index = jnp.arange(NX, dtype=jnp.int32)[:, None]
    level = 5 + 50 * row_index // NX
    rolled = jax.random.randint(folded, (NX, NY), 0, 100)
    return (rolled >= level).astype(jnp.int32)


def draw_land_sea(key, part):
    return wet_field(key)


def draw_courant_x(key, part):
    wet_cells = wet_field(key).astype(jnp.float32)
    uniform_part = jax.random.uniform(jax.random.fold_in(key, 21), (NX, NY), jnp.float32)
    coef = 0.05 + 0.4 * uniform_part
    beside = jnp.concatenate([wet_cells[1:], jnp.zeros((1, NY), jnp.float32)], 0)
    return coef * wet_cells * beside


def draw_courant_y(key, part):
    wet_cells = wet_field(key).astype(jnp.float32)
    uniform_part = jax.random.uniform(jax.random.fold_in(key, 22), (NX, NY), jnp.float32)
    coef = 0.05 + 0.4 * uniform_part
    beside = jnp.concatenate([wet_cells[:, 1:], jnp.zeros((NX, 1), jnp.float32)], 1)
    return coef * wet_cells * beside


def draw_tile_patches(key, part):
    blocks_x = NX // BS
    blocks_y = NY // BS
    slots_x = CX // BS + 1
    slots_y = CY // BS + 1
    shuffle = jax.random.permutation(jax.random.fold_in(key, 3), blocks_x * blocks_y).astype(jnp.int32)
    tile_rows = jnp.arange(TILES_X, dtype=jnp.int32)[:, None, None, None]
    tile_columns = jnp.arange(TILES_Y, dtype=jnp.int32)[None, :, None, None]
    local_rows = jnp.arange(slots_x, dtype=jnp.int32)[None, None, :, None]
    local_columns = jnp.arange(slots_y, dtype=jnp.int32)[None, None, None, :]
    block_row = (tile_rows * (CX // BS) + local_rows) % blocks_x
    block_column = (tile_columns * (CY // BS) + local_columns) % blocks_y
    return shuffle[block_row * blocks_y + block_column].reshape(TILES_X, TILES_Y, slots_x * slots_y)


def steps_of(key, extent, cuts, smallest, top_value):
    loudness, own = 1.0, jax.random.fold_in(key, 6)
    for axis_at, shards_of in cuts:
        steps = jnp.exp(jax.random.uniform(jax.random.fold_in(own, axis_at), (shards_of,), jnp.float32, smallest / len(cuts), top_value / len(cuts)))
        loudness = loudness * jnp.repeat(steps, extent[axis_at] // shards_of).reshape([-1 if axis == axis_at else 1 for axis in range(len(extent))])
    return loudness


def normal_values(stream_key, dims, width, most, shards=(), held_as=jnp.bfloat16):
    array = width * jax.random.normal(stream_key, dims, jnp.float32)
    if shards:
        array = array * steps_of(stream_key, dims, shards, -0.22, 0.18)
    return jnp.clip(array, -most, most).astype(held_as)


def setup_inputs(seed: int = 0) -> dict:
    arg_keys = jax.random.split(jax.random.key(seed), 10)
    return {
        "terminal_elevation": normal_values(arg_keys[0], (GAUGES, NX, NY), 1.0, 6.0, ((1, 4), (2, 8)), jnp.float32),
        "terminal_flux_x": normal_values(arg_keys[1], (GAUGES, NX, NY), 1.0, 6.0, ((1, 4), (2, 8)), jnp.float32),
        "terminal_flux_y": normal_values(arg_keys[2], (GAUGES, NX, NY), 1.0, 6.0, ((1, 4), (2, 8)), jnp.float32),
        "courant_x": draw_courant_x(jax.random.fold_in(arg_keys[9], 71), 0),
        "courant_y": draw_courant_y(jax.random.fold_in(arg_keys[9], 71), 0),
        "land_sea": draw_land_sea(jax.random.fold_in(arg_keys[9], 71), 0),
        "uplift": jnp.clip(jnp.exp(math.log(1.0) - 2.3025851 * jax.random.uniform(arg_keys[6], (NX, NY), jnp.float32) ** steps_of(arg_keys[6], (NX, NY), ((0, 4), (1, 8)), -0.2, 0.2)), 0.1, 1.0),
        "tile_patches": draw_tile_patches(jax.random.fold_in(arg_keys[9], 71), 0),
        "patch_home": jax.random.permutation(arg_keys[8], PATCHES).astype(jnp.int32),
    }


def advance_field(height, flux_x, flux_y, coef_x, coef_y, wet_cells):
    east_side = jnp.pad(height[1:], ((0, 1), (0, 0)))
    north_side = jnp.pad(height[:, 1:], ((0, 0), (0, 1)))
    fresh_x = flux_x + east_side - height
    fresh_y = flux_y + north_side - height
    along_x = coef_x * fresh_x
    along_y = coef_y * fresh_y
    west_side = jnp.pad(along_x[:-1], ((1, 0), (0, 0)))
    south_side = jnp.pad(along_y[:, :-1], ((0, 0), (1, 0)))
    return wet_cells * (height + along_x - west_side + along_y - south_side), fresh_x, fresh_y


def reference(terminal_elevation, terminal_flux_x, terminal_flux_y, courant_x, courant_y, land_sea, uplift, tile_patches, patch_home):
    wet_cells = land_sea.astype(jnp.float32)

    def one_gauge(fields):
        height, flux_x, flux_y = fields
        for iteration in range(ITERS):
            height, flux_x, flux_y = advance_field(height, flux_x, flux_y, courant_x, courant_y, wet_cells)
        return height

    adjoint = lax.map(one_gauge, (terminal_elevation, terminal_flux_x, terminal_flux_y))
    row_index = jnp.arange(NX, dtype=jnp.int32)
    column_index = jnp.arange(NY, dtype=jnp.int32)
    tile_x = row_index // CX
    tile_y = column_index // CY
    slot_x = (row_index % CX + BS // 2) // BS
    slot_y = (column_index % CY + BS // 2) // BS
    slot_index = slot_x[:, None] * (CY // BS + 1) + slot_y[None, :]
    owner_patch = tile_patches[tile_x[:, None], tile_y[None, :], slot_index]
    weight = wet_cells * uplift / BS
    flat_owner = owner_patch.reshape(-1)

    def gauge_sums(height):
        return jax.ops.segment_sum((weight * height).reshape(-1), flat_owner, num_segments=PATCHES)

    totals = lax.map(gauge_sums, adjoint)
    gradient = jnp.zeros((PATCHES, GAUGES), jnp.float32).at[patch_home].set(totals.T)
    return adjoint, gradient
```

```python
import jax
import jax.numpy as jnp
from jax import lax
from jax.experimental import pallas as pl
from jax.experimental.pallas import tpu as pltpu
from jax.sharding import PartitionSpec as P

BS = 64
ITERS = 8
LANES = 128
W = 8
GROUPS = LANES // W
F32 = jnp.float32
VMEM = pl.BlockSpec(memory_space=pltpu.VMEM)
SMEM = pl.BlockSpec(memory_space=pltpu.SMEM)
HBM = pl.BlockSpec(memory_space=pl.ANY)


def lanes_of(shape=(8, LANES)):
    return lax.broadcasted_iota(jnp.int32, shape, len(shape) - 1)


def roll(vector, distance):
    distance = distance % LANES
    return pltpu.roll(vector, distance, vector.ndim - 1) if distance else vector


def params(mebibytes):
    return pltpu.CompilerParams(vmem_limit_bytes=mebibytes * 2**20)


def tile(ref, row):
    return ref[pl.ds(row if isinstance(row, int) else pl.multiple_of(row, 8), 8), :]


def payload_layout(rows):
    heights = rows // GROUPS
    tiles = rows // 8 // GROUPS
    return (0, heights, 2 * heights, 2 * heights + tiles, 2 * heights + 2 * tiles)


def load_kernel(rows, h_hbm, x_hbm, y_hbm, cx_ref, cy_ref, wet_ref, h_out, d_out, even_out, odd_out, hb, xb, yb, sems):
    gauges = 8
    parts = 4
    size = rows // parts

    def piece(part, source, target, gauge):
        return pltpu.make_async_copy(
            source.at[pl.ds(gauge * rows + part * size, size)],
            target.at[pl.ds(part * size, size), gauge],
            sems.at[part],
        )

    for part in range(parts):
        for source, target in ((h_hbm, hb), (x_hbm, xb), (y_hbm, yb)):
            for gauge in range(gauges):
                piece(part, source, target, gauge).start()

    even = lax.rem(lax.axis_index("gy"), 2) == 0
    lane = lanes_of()
    group = lane // W
    at_h, at_d, at_cx, at_cy, at_g = payload_layout(rows)

    def put(place, to_left, to_right):
        even_out[place] = jnp.where(even, to_right, to_left)
        odd_out[place] = jnp.where(even, to_left, to_right)

    for ref, place in ((cx_ref, at_cx), (cy_ref, at_cy)):
        for p in range(rows // 8 // GROUPS):
            to_left = to_right = jnp.zeros((8, LANES), F32)
            for k in range(GROUPS):
                value = ref[pl.ds((p * GROUPS + k) * 8, 8), :]
                to_left = jnp.where(group == k, roll(value, W * k), to_left)
                to_right = jnp.where(group == k, roll(value, W * k + W), to_right)
            put(place + p, to_left, to_right)

    def block(m, above):
        lefts = [jnp.zeros((8, LANES), F32)] * 2
        rights = [jnp.zeros((8, LANES), F32)] * 2
        for k in range(GROUPS):
            r = m * GROUPS + k
            cx = cx_ref[pl.ds(r, 1), :]
            cy = cy_ref[pl.ds(r, 1), :]
            wet = wet_ref[pl.ds(r, 1), :].astype(F32)
            along_x = cx * xb[r]
            along_y = cy * yb[r]
            before_y = roll(along_y, 1)
            height = wet * hb[r]
            part = (along_x - above) + along_y
            divergence = part - jnp.where(lane == 0, 0.0, before_y)
            outgoing = jnp.where(lane == 0, -before_y, divergence)
            above = along_x
            h_out[r] = height
            d_out[r] = divergence
            mine = group == k
            lefts = [
                jnp.where(mine, roll(height, W * k), lefts[0]),
                jnp.where(mine, roll(divergence, W * k), lefts[1]),
            ]
            rights = [
                jnp.where(mine, roll(height, W * k + W), rights[0]),
                jnp.where(mine, roll(outgoing, W * k + W - 1), rights[1]),
            ]
        put(at_h + m, lefts[0], rights[0])
        put(at_d + m, lefts[1], rights[1])
        return above

    above = jnp.zeros((8, LANES), F32)
    blocks = size // GROUPS
    for part in range(parts):
        done = hb.at[pl.ds(0, 3 * size)] if 3 * size <= rows else None
        pltpu.make_async_copy(done, done, sems.at[part]).wait()
        above = lax.fori_loop(part * blocks, (part + 1) * blocks, block, above)
    h_out[rows] = jnp.zeros((8, LANES), F32)
    d_out[rows] = -above
    put(at_g, -above, roll(-above, W))


def row_step(h_in, d_in, h_out, d_out, cx_ref, cy_ref, r, height, before):
    following = h_in[r + 1]
    along_x = cx_ref[pl.ds(r, 1), :] * (following - height)
    along_y = cy_ref[pl.ds(r, 1), :] * (roll(height, LANES - 1) - height)
    divergence = d_in[r] + ((along_x - before) + (along_y - roll(along_y, 1)))
    d_out[r] = divergence
    h_out[r] = height + divergence
    return following, along_x


def sweep(rows, unroll, h_in, d_in, h_out, d_out, cx_ref, cy_ref):
    def block(b, carry):
        height, before = carry
        for k in range(unroll):
            height, before = row_step(
                h_in, d_in, h_out, d_out, cx_ref, cy_ref, b * unroll + k, height, before
            )
        return height, before

    lax.fori_loop(0, rows // unroll, block, (h_in[0], jnp.zeros((8, LANES), F32)))


def run_steps(rows, h_in, d_in, h_out, d_out, cx_ref, cy_ref):
    h_out[rows] = jnp.zeros((8, LANES), F32)
    sweep(rows, 16, h_in, d_in, h_out, d_out, cx_ref, cy_ref)

    def again(t, carry):
        sweep(rows, 16, h_out, d_out, h_out, d_out, cx_ref, cy_ref)
        return carry

    lax.fori_loop(1, ITERS, again, 0)


def center_kernel(rows, h_ref, d_ref, cx_ref, cy_ref, h_out, d_work):
    run_steps(rows, h_ref, d_ref, h_out, d_work, cx_ref, cy_ref)


def strip(lane, own, from_left, from_right):
    return jnp.where(
        lane >= LANES - 2 * W,
        own,
        jnp.where(lane < W, from_right, jnp.where(lane < 64, from_left, roll(own, 64))),
    )


def strip_divergence(lane, own, from_left, from_right):
    middle = jnp.where(lane >= 64, roll(own, 64), 0.0) + jnp.where(
        (lane > 64 - W) & (lane <= 64), from_left, 0.0
    )
    return jnp.where(lane >= LANES - 2 * W, own, jnp.where(lane < W, from_right, middle))


class Sides:
    def __init__(self, even_in, odd_in, even_out, odd_out):
        self.even = lax.rem(lax.axis_index("gy"), 2) == 0
        self.lane = lanes_of()
        self.refs = (even_in, odd_in, even_out, odd_out)

    def left(self, place):
        even_in, odd_in, _, _ = self.refs
        return jnp.where(self.even, odd_in[place], even_in[place])

    def right(self, place):
        even_in, odd_in, _, _ = self.refs
        return jnp.where(self.even, even_in[place], odd_in[place])

    def right_divergence(self, place):
        _, _, even_out, odd_out = self.refs
        sent = jnp.where(self.even, even_out[place], odd_out[place])
        return self.right(place) + jnp.where(self.lane % W == 0, roll(sent, -(W - 1)), 0.0)


def middle_kernel(rows, even_in, odd_in, even_out, odd_out, h_ref, d_ref, cx_ref, cy_ref, x_even, x_odd):
    side = Sides(even_in, odd_in, even_out, odd_out)
    lane, group = side.lane, side.lane // W
    at_h, at_d, at_cx, at_cy, at_g = payload_layout(rows)
    last_h, last_c = rows // GROUPS - 1, rows // 8 // GROUPS - 1
    even = lax.rem(lax.axis_index("gx"), 2) == 0

    def put(place, up, down):
        x_even[place] = jnp.where(even, down, up)
        x_odd[place] = jnp.where(even, up, down)

    for j in range(W):
        put(j, h_ref[j], h_ref[rows - W + j])
        put(W + j, d_ref[j], d_ref[rows - W + j])
    first = lane < 64
    put(
        2 * W,
        jnp.where(first, side.left(at_h), roll(side.right(at_h), 64)),
        jnp.where(first, roll(side.left(at_h + last_h), 64), side.right(at_h + last_h)),
    )
    put(
        2 * W + 1,
        jnp.where(first, side.left(at_d), roll(side.right_divergence(at_d), 64)),
        jnp.where(first, roll(side.left(at_d + last_h), 64), side.right_divergence(at_d + last_h)),
    )
    put(2 * W + 2, cx_ref[0:8, :], cx_ref[rows - 8 : rows, :])
    put(2 * W + 3, cy_ref[0:8, :], cy_ref[rows - 8 : rows, :])

    def gathered(pieces):
        result = pieces[0]
        for k, piece in enumerate(pieces[1:], 1):
            result = jnp.where(group == k, roll(piece, W * k), result)
        return result

    g_left, g_right = side.left(at_g), side.right(at_g)
    put(
        2 * W + 4,
        gathered([side.left(at_cx), side.right(at_cx), side.left(at_cy), side.right(at_cy), g_left, g_right]),
        gathered(
            [roll(side.left(at_cx + last_c), W), roll(side.right(at_cx + last_c), W)]
            + [roll(side.left(at_cy + last_c), W), roll(side.right(at_cy + last_c), W)]
            + [g_left, g_right]
        ),
    )
    put(2 * W + 5, d_ref[rows], d_ref[rows])


MESSAGE = 2 * W + 6


def strips_kernel(
    rows, even_in, odd_in, even_out, odd_out, h_ref, d_ref, cx_ref, cy_ref, done_ref, wet_ref, uplift_ref, lists_ref, home_ref,
    out_hbm, bh0, bd0, cbx, cby, hb, sums, homes, db, merged, sem,
):
    side = Sides(even_in, odd_in, even_out, odd_out)
    lane = side.lane
    at_h, at_d, at_cx, at_cy, at_g = payload_layout(rows)
    for ref, target, place in ((cx_ref, cbx, at_cx), (cy_ref, cby, at_cy)):
        for p in range(rows // 8 // GROUPS):
            left, right = side.left(place + p), side.right(place + p)
            for k in range(GROUPS):
                q = (p * GROUPS + k) * 8
                target[pl.ds(q, 8), :] = strip(
                    lane, ref[pl.ds(q, 8), :], roll(left, 64 - W - W * k), roll(right, -W * k)
                )

    def build(m, carry):
        h_left, h_right = side.left(at_h + m), side.right(at_h + m)
        d_left, d_right = side.left(at_d + m), side.right_divergence(at_d + m)
        for k in range(GROUPS):
            r = m * GROUPS + k
            bh0[r] = strip(lane, h_ref[r], roll(h_left, 64 - W - W * k), roll(h_right, -W * k))
            bd0[r] = strip_divergence(
                lane, d_ref[r], roll(d_left, 64 - W + 1 - W * k), roll(d_right, -W * k)
            )
        return carry

    lax.fori_loop(0, rows // GROUPS, build, 0)
    bh0[rows] = jnp.zeros((8, LANES), F32)
    bd0[rows] = strip(lane, d_ref[rows], roll(side.left(at_g), 64 - W), side.right(at_g))
    run_steps(rows, bh0, bd0, hb, db, cbx, cby)

    def weigh(b, total):
        for k in range(8):
            r = b * 8 + k
            value = merge(lane, done_ref[r], hb[r])
            merged[r] = value
            weight = wet_ref[pl.ds(r, 1), :].astype(F32) * uplift_ref[pl.ds(r, 1), :] * (1.0 / BS)
            total = total + weight * value
        return total

    bounds = slot_bounds(rows)
    for u in range(len(bounds) - 1):
        low, high = max(bounds[u], W) // 8, min(bounds[u + 1], rows - W) // 8
        sums[u] = lax.fori_loop(low, high, weigh, jnp.zeros((8, LANES), F32))
    count = rows - 2 * W
    copies = [
        pltpu.make_async_copy(merged.at[pl.ds(W, count), g], out_hbm.at[pl.ds(g * rows + W, count)], sem)
        for g in range(8)
    ]
    for copy in copies:
        copy.start()

    tile_at = lax.axis_index("gx") * lax.axis_size("gy") + lax.axis_index("gy")
    slots = homes.shape[0]
    for s in range(slots):
        patch = lists_ref[tile_at * slots + s]
        homes[pl.ds(s, 1), :] = jnp.full((1, LANES), home_ref[patch], jnp.int32)
    for copy in copies:
        copy.wait()


def merge(lane, center, strips):
    return jnp.where(lane < W, roll(strips, 64), jnp.where(lane >= LANES - W, strips, center))


def slot_bounds(length):
    return [0] + list(range(BS // 2, length, BS)) + [length]


def bands_kernel(
    rows, x_even_in, x_odd_in, h_ref, d_ref, cx_ref, cy_ref, bh0, bd0, cbx, cby, done_wet, uplift_ref, sums_ref, homes_ref, out_in,
    out_hbm, message, hs, ds, cxs, cys, edge, sem,
):
    lane = lanes_of()
    even = lax.rem(lax.axis_index("gx"), 2) == 0
    depth = 3 * W

    def above(place):
        return jnp.where(even, x_odd_in[place], x_even_in[place])

    def below(place):
        return jnp.where(even, x_even_in[place], x_odd_in[place])

    for band, (got, halo_at, own_at, own_row) in enumerate(
        ((above, 0, W, 0), (below, 2 * W, 0, rows - 2 * W))
    ):
        center, side = 2 * band, 2 * band + 1
        packed_h, packed_d, packed_c = got(2 * W), got(2 * W + 1), got(2 * W + 4)
        for j in range(W):
            height, divergence = got(j), got(W + j)
            hs[center, halo_at + j] = height
            ds[center, halo_at + j] = divergence
            hs[side, halo_at + j] = strip(
                lane, height, roll(packed_h, 64 - W - W * j), roll(packed_h, -64 - W * j)
            )
            ds[side, halo_at + j] = strip_divergence(
                lane, divergence, roll(packed_d, 64 - W + 1 - W * j), roll(packed_d, -64 - W * j)
            )
        for c, (ref, mine, strips) in enumerate(((cxs, cx_ref, cbx), (cys, cy_ref, cby))):
            value = got(2 * W + 2 + c)
            ref[center, pl.ds(halo_at, W), :] = value
            ref[side, pl.ds(halo_at, W), :] = strip(
                lane, value, roll(packed_c, 64 - W - 2 * W * c), roll(packed_c, -W - 2 * W * c)
            )
            ref[center, pl.ds(own_at, 2 * W), :] = mine[pl.ds(own_row, 2 * W), :]
            ref[side, pl.ds(own_at, 2 * W), :] = strips[pl.ds(own_row, 2 * W), :]
        for j in range(2 * W):
            hs[center, own_at + j] = h_ref[own_row + j]
            ds[center, own_at + j] = d_ref[own_row + j]
            hs[side, own_at + j] = bh0[own_row + j]
            ds[side, own_at + j] = bd0[own_row + j]
        if band == 0:
            flux = got(2 * W + 5)
            ds[center, W] = ds[center, W] + flux
            ds[side, W] = ds[side, W] + strip(
                lane, flux, roll(packed_c, 64 - W - 4 * W), roll(packed_c, -5 * W)
            )
        else:
            ds[center, 2 * W] = ds[center, 2 * W] + d_ref[rows]
            ds[side, 2 * W] = ds[side, 2 * W] + bd0[rows]
        for b in (center, side):
            hs[b, depth] = jnp.zeros((8, LANES), F32)

    def step(t, carry):
        state = [(hs[b, 0], jnp.zeros((8, LANES), F32)) for b in range(4)]
        for r in range(depth):
            for b in range(4):
                h_b, d_b = hs.at[b], ds.at[b]
                state[b] = row_step(h_b, d_b, h_b, d_b, cxs.at[b], cys.at[b], r, *state[b])
        return carry

    lax.fori_loop(0, ITERS, step, 0)

    bounds = slot_bounds(rows)
    slots_x = len(bounds) - 1
    totals = [sums_ref[u] for u in range(slots_x)]
    for band, first in ((0, 0), (1, rows - W)):
        slot = 0 if band == 0 else slots_x - 1
        for j in range(W):
            value = merge(lane, hs[2 * band, W + j], hs[2 * band + 1, W + j])
            edge[band * W + j] = value
            weight = done_wet[pl.ds(first + j, 1), :].astype(F32) * uplift_ref[pl.ds(first + j, 1), :] * (1.0 / BS)
            totals[slot] = totals[slot] + weight * value
    copies = [
        pltpu.make_async_copy(
            edge.at[pl.ds(band * W, W), g], out_hbm.at[pl.ds(g * rows + first, W)], sem
        )
        for band, first in ((0, 0), (1, rows - W))
        for g in range(8)
    ]
    for copy in copies:
        copy.start()

    column_bounds = slot_bounds(LANES)
    slots_y = len(column_bounds) - 1
    devices = message.shape[0]
    gauge = lax.broadcasted_iota(jnp.int32, (8, LANES), 0)
    shape = (devices, LANES)
    here = lanes_of(shape)
    per_device = 8
    home_of = jnp.where(
        here < per_device * 8,
        lax.broadcasted_iota(jnp.int32, shape, 0) * per_device + here // 8,
        -1,
    )
    built = jnp.zeros(shape, F32)
    for u in range(slots_x):
        for w in range(slots_y):
            inside = (lane >= column_bounds[w]) & (lane < column_bounds[w + 1])
            total = jnp.sum(jnp.where(inside, totals[u], 0.0), axis=1, keepdims=True)
            spread = jnp.sum(jnp.where(lane % 8 == gauge, total, 0.0), axis=0, keepdims=True)
            home = homes_ref[pl.ds(u * slots_y + w, 1), :]
            built = built + jnp.where(home_of == home, spread, 0.0)
    message[...] = built
    for copy in copies:
        copy.wait()


def final_kernel(received, gradient):
    total = jnp.sum(received[...], axis=0, keepdims=True)
    lane = lanes_of()
    row = lax.broadcasted_iota(jnp.int32, (8, LANES), 0)
    result = jnp.zeros((8, LANES), F32)
    for k in range(8):
        result = jnp.where(row == k, roll(jnp.broadcast_to(total, (8, LANES)), -8 * k), result)
    gradient[...] = result[:, :8]


def pairs(axis, first):
    return [
        pair
        for i in range(first, lax.axis_size(axis) - 1, 2)
        for pair in ((i, i + 1), (i + 1, i))
    ]


def shaped(*shape, dtype=F32):
    return jax.ShapeDtypeStruct(shape, dtype)


def bind(kernel, rows):
    def bound(*refs):
        kernel(rows, *refs)

    return bound


def body(
    terminal_elevation,
    terminal_flux_x,
    terminal_flux_y,
    courant_x,
    courant_y,
    land_sea,
    uplift,
    tile_patches,
    patch_home,
):
    gauges, rows, columns = terminal_elevation.shape
    flat = (gauges * rows, columns)
    layers = (rows + 8, gauges, columns)
    devices = lax.axis_size("gx") * lax.axis_size("gy")
    slots = tile_patches.shape[2]
    slots_x = len(slot_bounds(rows)) - 1
    vectors = payload_layout(rows)[-1] + 1
    field = pltpu.VMEM((rows, gauges, columns), F32)
    work = pltpu.VMEM(layers, F32)

    height, divergence, even_out, odd_out = pl.pallas_call(
        bind(load_kernel, rows),
        out_shape=(shaped(*layers), shaped(*layers), shaped(vectors, 8, columns), shaped(vectors, 8, columns)),
        in_specs=[HBM] * 3 + [VMEM] * 3,
        out_specs=(VMEM,) * 4,
        scratch_shapes=[field] * 3 + [pltpu.SemaphoreType.DMA((4,))],
        compiler_params=params(LOAD_MIB),
        name="load",
    )(
        terminal_elevation.reshape(flat),
        terminal_flux_x.reshape(flat),
        terminal_flux_y.reshape(flat),
        courant_x,
        courant_y,
        land_sea,
    )
    even_in = lax.ppermute(even_out, "gy", pairs("gy", 0))
    odd_in = lax.ppermute(odd_out, "gy", pairs("gy", 1))

    row_ops = rows * ITERS * 8 * columns
    center = pl.pallas_call(
        bind(center_kernel, rows),
        out_shape=shaped(*layers),
        in_specs=[VMEM] * 4,
        out_specs=VMEM,
        scratch_shapes=[work],
        compiler_params=params(8),
        cost_estimate=pl.CostEstimate(flops=row_ops * 9, bytes_accessed=2**20, transcendentals=0),
        name="center",
    )(height, divergence, courant_x, courant_y)

    x_even_out, x_odd_out = pl.pallas_call(
        bind(middle_kernel, rows),
        out_shape=(shaped(MESSAGE, 8, columns),) * 2,
        in_specs=[VMEM] * 8,
        out_specs=(VMEM,) * 2,
        compiler_params=params(4),
        name="middle",
    )(even_in, odd_in, even_out, odd_out, height, divergence, courant_x, courant_y)
    x_even_in = lax.ppermute(x_even_out, "gx", pairs("gx", 0))
    x_odd_in = lax.ppermute(x_odd_out, "gx", pairs("gx", 1))

    partial_out, bh0, bd0, cbx, cby, _, sums, homes = pl.pallas_call(
        bind(strips_kernel, rows),
        out_shape=(
            shaped(*flat), shaped(*layers), shaped(*layers), shaped(rows, columns), shaped(rows, columns),
            shaped(*layers), shaped(slots_x, 8, columns), shaped(slots, columns, dtype=jnp.int32),
        ),
        in_specs=[VMEM] * 11 + [SMEM] * 2,
        out_specs=(HBM,) + (VMEM,) * 7,
        scratch_shapes=[work, field, pltpu.SemaphoreType.DMA],
        compiler_params=params(8),
        cost_estimate=pl.CostEstimate(flops=row_ops * 9, bytes_accessed=2**20, transcendentals=0),
        name="strips",
    )(
        even_in, odd_in, even_out, odd_out, height, divergence, courant_x, courant_y, center,
        land_sea, uplift, tile_patches.reshape(-1), patch_home,
    )

    depth = 3 * W
    out, message = pl.pallas_call(
        bind(bands_kernel, rows),
        out_shape=(shaped(*flat), shaped(devices, columns)),
        in_specs=[VMEM] * 14 + [HBM],
        out_specs=(HBM, VMEM),
        input_output_aliases={14: 0},
        scratch_shapes=[
            pltpu.VMEM((4, depth + 8, 8, columns), F32),
            pltpu.VMEM((4, depth + 8, 8, columns), F32),
            pltpu.VMEM((4, depth, columns), F32),
            pltpu.VMEM((4, depth, columns), F32),
            pltpu.VMEM((2 * W, 8, columns), F32),
            pltpu.SemaphoreType.DMA,
        ],
        compiler_params=params(4),
        name="bands",
    )(
        x_even_in, x_odd_in, height, divergence, courant_x, courant_y, bh0, bd0, cbx, cby,
        land_sea, uplift, sums, homes, partial_out,
    )
    received = lax.all_to_all(message, ("gx", "gy"), 0, 0, tiled=True)
    gradient = pl.pallas_call(
        final_kernel,
        out_shape=shaped(patch_home.shape[0] // devices, gauges),
        in_specs=[VMEM],
        out_specs=VMEM,
        name="final",
    )(received)
    return (out.reshape(gauges, rows, columns), gradient)


LOAD_MIB = 8


def solution(mesh):
    in_specs = (
        P(None, "gx", "gy"),
        P(None, "gx", "gy"),
        P(None, "gx", "gy"),
        P("gx", "gy"),
        P("gx", "gy"),
        P("gx", "gy"),
        P("gx", "gy"),
        P(),
        P(),
    )
    out_specs = (P(None, "gx", "gy"), P(("gx", "gy"), None))
    return jax.shard_map(body, mesh=mesh, in_specs=in_specs, out_specs=out_specs, check_vma=False)
```

```python
import jax
import jax.numpy as jnp
from jax import lax
from jax.experimental import pallas as pl
from jax.experimental.pallas import tpu as pltpu
from jax.sharding import PartitionSpec as P

BS = 64
ITERS = 8
LANES = 128
W = 8
GROUPS = LANES // W
F32 = jnp.float32
VMEM = pl.BlockSpec(memory_space=pltpu.VMEM)
SMEM = pl.BlockSpec(memory_space=pltpu.SMEM)
HBM = pl.BlockSpec(memory_space=pl.ANY)


def lanes_of(shape=(8, LANES)):
    return lax.broadcasted_iota(jnp.int32, shape, len(shape) - 1)


def roll(vector, distance):
    distance = distance % LANES
    return pltpu.roll(vector, distance, vector.ndim - 1) if distance else vector


def params(mebibytes):
    return pltpu.CompilerParams(vmem_limit_bytes=mebibytes * 2**20)


def tile(ref, row):
    return ref[pl.ds(row if isinstance(row, int) else pl.multiple_of(row, 8), 8), :]


def payload_layout(rows):
    heights = rows // GROUPS
    tiles = rows // 8 // GROUPS
    return (0, heights, 2 * heights, 2 * heights + tiles, 2 * heights + 2 * tiles)


def advance(items, lag):
    live = {}
    written = {}
    for i in range(-2 * lag, len(items)):
        if i + 2 * lag < len(items):
            h_in, _, _, _, _, _, r, has_above, below = items[i + 2 * lag]
            assert written.get((id(h_in), r), -(10**9)) < i
            height = h_in[r]
            live[i + 2 * lag] = [
                height,
                roll(height, LANES - 1),
                h_in[r - 1] if has_above else None,
                h_in[r + 1] if below == "row" else None,
                None,
                None,
            ]
        if 0 <= i + lag < len(items):
            state = live[i + lag]
            coef_y, r = items[i + lag][5], items[i + lag][6]
            along = coef_y[pl.ds(r, 1), :] * (state[1] - state[0])
            state[4] = along
            state[5] = roll(along, 1)
        if i >= 0:
            h_in, d_in, h_out, d_out, coef_x, _, r, has_above, below = items[i]
            height, _, above, under, along, along_before = live.pop(i)
            if below == "item":
                under = live[i + 1][0]
            if has_above:
                before = coef_x[pl.ds(r - 1, 1), :] * (height - above)
            elif i == 0 or items[i - 1][8] != "item":
                before = None
            flux = coef_x[pl.ds(r, 1), :] * ((under - height) if under is not None else -height)
            change = along - along_before + (flux if before is None else flux - before)
            divergence = d_in[r] + change
            d_out[r] = divergence
            h_out[r] = height + divergence
            written[(id(h_out), r)] = i
            before = flux


def rows_of(count, refs):
    return [refs + (r, False, "item" if r + 1 < count else None) for r in range(count)]


def run_steps(count, steps, unroll, first, then, lag):
    if first is not None:
        head = rows_of(count, first)
        for _ in range(unroll - 1):
            head = head + rows_of(count, then)
        advance(head, lag)

    def again(t, carry):
        advance(rows_of(count, then) * unroll, lag)
        return carry

    rounds = steps // unroll - (first is not None)
    if rounds == 1:
        again(0, 0)
    elif rounds:
        lax.fori_loop(0, rounds, again, 0)


def load_kernel(
    rows, h_hbm, x_hbm, y_hbm, cx_hbm, cy_hbm, wet_hbm,
    h_out, d_out, even_out, odd_out, cx_ref, cy_ref, hb, xb, yb, wet_ref, sems,
):
    gauges = 8
    parts = 4
    size = rows // parts
    plain = [
        pltpu.make_async_copy(source, target, sems.at[parts + i])
        for i, (source, target) in enumerate(((cx_hbm, cx_ref), (cy_hbm, cy_ref), (wet_hbm, wet_ref)))
    ]
    for copy in plain:
        copy.start()
    for part in range(parts):
        for source, target in ((y_hbm, yb), (x_hbm, xb), (h_hbm, hb)):
            for gauge in range(gauges):
                pltpu.make_async_copy(
                    source.at[pl.ds(gauge * rows + part * size, size)],
                    target.at[pl.ds(part * size, size), gauge],
                    sems.at[part],
                ).start()

    even = lax.rem(lax.axis_index("gy"), 2) == 0
    lane = lanes_of()
    group = lane // W
    at_h, at_d, at_cx, at_cy, at_g = payload_layout(rows)

    def put(place, to_left, to_right):
        even_out[place] = jnp.where(even, to_right, to_left)
        odd_out[place] = jnp.where(even, to_left, to_right)

    for copy in plain:
        copy.wait()
    for ref, place in ((cx_ref, at_cx), (cy_ref, at_cy)):
        for p in range(rows // 8 // GROUPS):
            to_left = to_right = jnp.zeros((8, LANES), F32)
            for k in range(GROUPS):
                value = ref[pl.ds((p * GROUPS + k) * 8, 8), :]
                to_left = jnp.where(group == k, roll(value, W * k), to_left)
                to_right = jnp.where(group == k, roll(value, W * k + W), to_right)
            put(place + p, to_left, to_right)

    state = {}

    def early(r):
        along_y = cy_ref[pl.ds(r, 1), :] * yb[r]
        state[r] = (along_y, roll(along_y, 1))

    def late(r, above, sides):
        along_y, before_y = state.pop(r)
        along_x = cx_ref[pl.ds(r, 1), :] * xb[r]
        height = wet_ref[pl.ds(r, 1), :].astype(F32) * hb[r]
        part = along_y + along_x if above is None else along_y + (along_x - above)
        divergence = part - jnp.where(lane == 0, 0.0, before_y)
        outgoing = jnp.where(lane == 0, -before_y, divergence)
        h_out[r] = height
        d_out[r] = divergence
        k = r % GROUPS
        mine = group == k
        new = (
            roll(height, W * k),
            roll(divergence, W * k),
            roll(height, W * k + W),
            roll(outgoing, W * k + W - 1),
        )
        sides = new if k == 0 else tuple(jnp.where(mine, n, s) for n, s in zip(new, sides))
        if k == GROUPS - 1:
            put(at_h + r // GROUPS, sides[0], sides[2])
            put(at_d + r // GROUPS, sides[1], sides[3])
        return along_x, sides

    above, sides = None, None
    lag = 16
    for part in range(parts):
        done = hb.at[pl.ds(0, 3 * size)]
        pltpu.make_async_copy(done, done, sems.at[part]).wait()
        low, high = part * size, (part + 1) * size
        for r in range(low - lag, high):
            if r + lag < high:
                early(r + lag)
            if r >= low:
                above, sides = late(r, above, sides)
    d_out[rows] = -above
    put(at_g, -above, roll(-above, W))


def center_first_kernel(rows, steps, h_ref, d_ref, cx_ref, cy_ref, h_out, d_out, token):
    first = (h_ref, d_ref, h_out, d_out, cx_ref, cy_ref)
    then = (h_out, d_out, h_out, d_out, cx_ref, cy_ref)
    run_steps(rows, steps, 2, first, then, 24)
    token[...] = jnp.zeros((8, LANES), F32)


def center_second_kernel(rows, steps, h_ref, d_ref, cx_ref, cy_ref, h_out, d_work):
    first = (h_ref, d_ref, h_out, d_work, cx_ref, cy_ref)
    then = (h_out, d_work, h_out, d_work, cx_ref, cy_ref)
    run_steps(rows, steps, 2, first, then, 24)


SECOND = 32


def strip(lane, own, from_left, from_right):
    return jnp.where(
        lane >= LANES - 2 * W,
        own,
        jnp.where(lane < W, from_right, jnp.where(lane < 64, from_left, roll(own, 64))),
    )


def strip_divergence(lane, own, from_left, from_right):
    middle = jnp.where(lane >= 64, roll(own, 64), 0.0) + jnp.where(
        (lane > 64 - W) & (lane <= 64), from_left, 0.0
    )
    return jnp.where(lane >= LANES - 2 * W, own, jnp.where(lane < W, from_right, middle))


def second_lanes(lane):
    return ((lane >= 16) & (lane < 40)) | ((lane >= 88) & (lane < 112))


def merge(lane, center, packed, lower):
    shift = SECOND if lower else 0
    left, right = roll(packed, 64 - shift), roll(packed, -shift)
    return jnp.where(lane < W, left, jnp.where(lane >= LANES - W, right, center))


class Sides:
    def __init__(self, even_in, odd_in, even_out, odd_out):
        self.even = lax.rem(lax.axis_index("gy"), 2) == 0
        self.lane = lanes_of()
        self.refs = (even_in, odd_in, even_out, odd_out)

    def left(self, place):
        even_in, odd_in, _, _ = self.refs
        return jnp.where(self.even, odd_in[place], even_in[place])

    def right(self, place):
        even_in, odd_in, _, _ = self.refs
        return jnp.where(self.even, even_in[place], odd_in[place])

    def right_divergence(self, place):
        _, _, even_out, odd_out = self.refs
        sent = jnp.where(self.even, even_out[place], odd_out[place])
        return self.right(place) + jnp.where(self.lane % W == 0, roll(sent, -(W - 1)), 0.0)


def middle_kernel(rows, even_in, odd_in, even_out, odd_out, h_ref, d_ref, cx_ref, cy_ref, token, x_even, x_odd):
    side = Sides(even_in, odd_in, even_out, odd_out)
    lane, group = side.lane, side.lane // W
    at_h, at_d, at_cx, at_cy, at_g = payload_layout(rows)
    last_h, last_c = rows // GROUPS - 1, rows // 8 // GROUPS - 1
    even = lax.rem(lax.axis_index("gx"), 2) == 0

    def put(place, up, down):
        x_even[place] = jnp.where(even, down, up)
        x_odd[place] = jnp.where(even, up, down)

    for j in range(W):
        put(j, h_ref[j], h_ref[rows - W + j])
        put(W + j, d_ref[j], d_ref[rows - W + j])
    first = lane < 64
    put(
        2 * W,
        jnp.where(first, side.left(at_h), roll(side.right(at_h), 64)),
        jnp.where(first, roll(side.left(at_h + last_h), 64), side.right(at_h + last_h)),
    )
    put(
        2 * W + 1,
        jnp.where(first, side.left(at_d), roll(side.right_divergence(at_d), 64)),
        jnp.where(first, roll(side.left(at_d + last_h), 64), side.right_divergence(at_d + last_h)),
    )
    put(2 * W + 2, cx_ref[0:8, :], cx_ref[rows - 8 : rows, :])
    put(2 * W + 3, cy_ref[0:8, :], cy_ref[rows - 8 : rows, :])

    def gathered(pieces):
        result = pieces[0]
        for k, piece in enumerate(pieces[1:], 1):
            result = jnp.where(group == k, roll(piece, W * k), result)
        return result

    g_left, g_right = side.left(at_g), side.right(at_g)
    put(
        2 * W + 4,
        gathered([side.left(at_cx), side.right(at_cx), side.left(at_cy), side.right(at_cy), g_left, g_right]),
        gathered(
            [roll(side.left(at_cx + last_c), W), roll(side.right(at_cx + last_c), W)]
            + [roll(side.left(at_cy + last_c), W), roll(side.right(at_cy + last_c), W)]
            + [g_left, g_right]
        ),
    )
    put(2 * W + 5, d_ref[rows], d_ref[rows])


MESSAGE = 2 * W + 6


def strips_kernel(
    rows, even_in, odd_in, even_out, odd_out, h_ref, d_ref, cx_ref, cy_ref, done_ref, wet_ref, uplift_ref, lists_ref, home_ref,
    out_hbm, bh0, bd0, cbx, cby, sums, homes, hb, db, merged, lefts, rights, sem,
):
    side = Sides(even_in, odd_in, even_out, odd_out)
    lane = side.lane
    second = second_lanes(lane)
    at_h, at_d, at_cx, at_cy, at_g = payload_layout(rows)
    count = rows // 2 + W
    offset = rows // 2 - W
    for place in range(at_g + 1):
        lefts[place] = side.left(place)
        rights[place] = side.right_divergence(place) if at_d <= place < at_cx else side.right(place)

    for ref, target, place in ((cx_ref, cbx, at_cx), (cy_ref, cby, at_cy)):

        def strip_tile(row):
            p, k = divmod(row // 8, GROUPS)
            own = ref[pl.ds(row, 8), :]
            return strip(
                lane, own, roll(lefts[place + p], 64 - W - W * k), roll(rights[place + p], -W * k)
            )

        for row in range(0, count, 8):
            target[pl.ds(row, 8), :] = jnp.where(
                second, roll(strip_tile(row + offset), SECOND), strip_tile(row)
            )

    def height_strip(row):
        m, k = divmod(row, GROUPS)
        return strip(
            lane, h_ref[row], roll(lefts[at_h + m], 64 - W - W * k), roll(rights[at_h + m], -W * k)
        )

    def divergence_strip(row):
        m, k = divmod(row, GROUPS)
        left, right = roll(lefts[at_d + m], 64 - W + 1 - W * k), roll(rights[at_d + m], -W * k)
        return strip_divergence(lane, d_ref[row], left, right)

    for row in range(count):
        bh0[row] = jnp.where(second, roll(height_strip(row + offset), SECOND), height_strip(row))
        bd0[row] = jnp.where(second, roll(divergence_strip(row + offset), SECOND), divergence_strip(row))
    bd0[count] = strip(lane, d_ref[rows], roll(lefts[at_g], 64 - W), rights[at_g])
    first = (bh0, bd0, hb, db, cbx, cby)
    then = (hb, db, hb, db, cbx, cby)
    run_steps(count, ITERS, 2, first, then, 24)

    bounds = slot_bounds(rows)
    for u in range(len(bounds) - 1):
        total = jnp.zeros((8, LANES), F32)
        for r in range(max(bounds[u], W), min(bounds[u + 1], rows - W)):
            lower = r >= rows // 2
            value = merge(lane, done_ref[r], hb[r - offset if lower else r], lower)
            merged[r] = value
            weight = wet_ref[pl.ds(r, 1), :].astype(F32) * uplift_ref[pl.ds(r, 1), :] * (1.0 / BS)
            total = total + weight * value
        sums[u] = total
    inner = rows - 2 * W
    copies = [
        pltpu.make_async_copy(merged.at[pl.ds(W, inner), g], out_hbm.at[pl.ds(g * rows + W, inner)], sem)
        for g in range(8)
    ]
    for copy in copies:
        copy.start()

    tile_at = lax.axis_index("gx") * lax.axis_size("gy") + lax.axis_index("gy")
    slots = homes.shape[0]
    for s in range(slots):
        patch = lists_ref[tile_at * slots + s]
        homes[pl.ds(s, 1), :] = jnp.full((1, LANES), home_ref[patch], jnp.int32)
    for copy in copies:
        copy.wait()


def slot_bounds(length):
    return [0] + list(range(BS // 2, length, BS)) + [length]


def bands_kernel(
    rows, x_even_in, x_odd_in, h_ref, d_ref, cx_ref, cy_ref, bh0, bd0, cbx, cby, done_wet, uplift_ref, sums_ref, homes_ref, out_in,
    out_hbm, message, hs, ds, cxs, cys, edge, sem,
):
    lane = lanes_of()
    second = second_lanes(lane)
    even = lax.rem(lax.axis_index("gx"), 2) == 0
    depth = 3 * W
    count = rows // 2 + W

    def above(place):
        return jnp.where(even, x_odd_in[place], x_even_in[place])

    def below(place):
        return jnp.where(even, x_even_in[place], x_odd_in[place])

    def both(upper, lower):
        return jnp.where(second, lower, upper)

    top, bottom, strips = 0, 1, 2
    for c, (ref, mine, packed) in enumerate(((cxs, cx_ref, cbx), (cys, cy_ref, cby))):
        halos = []
        for got in (above, below):
            value, corner = got(2 * W + 2 + c), got(2 * W + 4)
            halos.append(
                (
                    value,
                    strip(
                        lane, value, roll(corner, 64 - W - 2 * W * c), roll(corner, -W - 2 * W * c)
                    ),
                )
            )
        ref[top, 0:W, :] = halos[0][0]
        ref[top, W:depth, :] = mine[0 : 2 * W, :]
        ref[bottom, 0 : 2 * W, :] = mine[rows - 2 * W : rows, :]
        ref[bottom, 2 * W : depth, :] = halos[1][0]
        ref[strips, 0:W, :] = both(halos[0][1], packed[count - 2 * W : count - W, :])
        ref[strips, W : 2 * W, :] = both(packed[0:W, :], packed[count - W : count, :])
        ref[strips, 2 * W : depth, :] = both(packed[W : 2 * W, :], roll(halos[1][1], SECOND))

    def halo_strips(got, j):
        packed_h, packed_d = got(2 * W), got(2 * W + 1)
        return (
            strip(lane, got(j), roll(packed_h, 64 - W - W * j), roll(packed_h, -64 - W * j)),
            strip_divergence(
                lane, got(W + j), roll(packed_d, 64 - W + 1 - W * j), roll(packed_d, -64 - W * j)
            ),
        )

    flux, corner = above(2 * W + 5), above(2 * W + 4)
    flux_strip = strip(lane, flux, roll(corner, 64 - W - 4 * W), roll(corner, -5 * W))
    for j in range(W):
        upper, lower = halo_strips(above, j), halo_strips(below, j)
        h_last, d_last = roll(lower[0], SECOND), roll(lower[1], SECOND)
        d_first, d_below = bd0[j], below(W + j)
        d_top = d_ref[j]
        if j == 0:
            d_first = d_first + flux_strip
            d_top = d_top + flux
            d_below = d_below + d_ref[rows]
            d_last = d_last + roll(bd0[count], SECOND)
        hs[top, j], ds[top, j] = above(j), above(W + j)
        hs[top, W + j], ds[top, W + j] = h_ref[j], d_top
        hs[top, 2 * W + j], ds[top, 2 * W + j] = h_ref[W + j], d_ref[W + j]
        low = rows - 2 * W + j
        hs[bottom, j], ds[bottom, j] = h_ref[low], d_ref[low]
        hs[bottom, W + j], ds[bottom, W + j] = h_ref[low + W], d_ref[low + W]
        hs[bottom, 2 * W + j], ds[bottom, 2 * W + j] = below(j), d_below
        low = count - 2 * W + j
        hs[strips, j], ds[strips, j] = both(upper[0], bh0[low]), both(upper[1], bd0[low])
        hs[strips, W + j] = both(bh0[j], bh0[low + W])
        ds[strips, W + j] = both(d_first, bd0[low + W])
        hs[strips, 2 * W + j] = both(bh0[W + j], h_last)
        ds[strips, 2 * W + j] = both(bd0[W + j], d_last)

    views = [(hs.at[b], ds.at[b], hs.at[b], ds.at[b], cxs.at[b], cys.at[b]) for b in range(3)]
    items = []
    for t in range(1, ITERS + 1):
        low, high = t, depth - t
        for view in views:
            for r in range(low, high):
                items.append(view + (r, r == low, "item" if r + 1 < high else "row"))
    advance(items, 8)

    bounds = slot_bounds(rows)
    slots_x = len(bounds) - 1
    totals = [sums_ref[u] for u in range(slots_x)]
    for band, first in ((top, 0), (bottom, rows - W)):
        slot = 0 if band == top else slots_x - 1
        for j in range(W):
            value = merge(lane, hs[band, W + j], hs[strips, W + j], band == bottom)
            edge[band * W + j] = value
            weight = done_wet[pl.ds(first + j, 1), :].astype(F32) * uplift_ref[pl.ds(first + j, 1), :] * (1.0 / BS)
            totals[slot] = totals[slot] + weight * value
    copies = [
        pltpu.make_async_copy(
            edge.at[pl.ds(band * W, W), g], out_hbm.at[pl.ds(g * rows + first, W)], sem
        )
        for band, first in ((0, 0), (1, rows - W))
        for g in range(8)
    ]
    for copy in copies:
        copy.start()

    column_bounds = slot_bounds(LANES)
    slots_y = len(column_bounds) - 1
    devices = message.shape[0]
    gauge = lax.broadcasted_iota(jnp.int32, (8, LANES), 0)
    shape = (devices, LANES)
    here = lanes_of(shape)
    per_device = 8
    home_of = jnp.where(
        here < per_device * 8,
        lax.broadcasted_iota(jnp.int32, shape, 0) * per_device + here // 8,
        -1,
    )
    built = jnp.zeros(shape, F32)
    for u in range(slots_x):
        for w in range(slots_y):
            inside = (lane >= column_bounds[w]) & (lane < column_bounds[w + 1])
            total = jnp.sum(jnp.where(inside, totals[u], 0.0), axis=1, keepdims=True)
            spread = jnp.sum(jnp.where(lane % 8 == gauge, total, 0.0), axis=0, keepdims=True)
            home = homes_ref[pl.ds(u * slots_y + w, 1), :]
            built = built + jnp.where(home_of == home, spread, 0.0)
    message[...] = built
    for copy in copies:
        copy.wait()


def final_kernel(received, gradient):
    total = jnp.sum(received[...], axis=0, keepdims=True)
    lane = lanes_of()
    row = lax.broadcasted_iota(jnp.int32, (8, LANES), 0)
    result = jnp.zeros((8, LANES), F32)
    for k in range(8):
        result = jnp.where(row == k, roll(jnp.broadcast_to(total, (8, LANES)), -8 * k), result)
    gradient[...] = result[:, :8]


def pairs(axis, first):
    return [
        pair
        for i in range(first, lax.axis_size(axis) - 1, 2)
        for pair in ((i, i + 1), (i + 1, i))
    ]


def in_hbm(array):
    return pltpu.with_memory_space_constraint(array, pltpu.HBM)


def shaped(*shape, dtype=F32):
    return jax.ShapeDtypeStruct(shape, dtype)


def bind(kernel, *sizes):
    def bound(*refs):
        kernel(*sizes, *refs)

    return bound


def body(
    terminal_elevation,
    terminal_flux_x,
    terminal_flux_y,
    courant_x,
    courant_y,
    land_sea,
    uplift,
    tile_patches,
    patch_home,
):
    gauges, rows, columns = terminal_elevation.shape
    flat = (gauges * rows, columns)
    layers = (rows + 8, gauges, columns)
    devices = lax.axis_size("gx") * lax.axis_size("gy")
    slots = tile_patches.shape[2]
    slots_x = len(slot_bounds(rows)) - 1
    vectors = payload_layout(rows)[-1] + 1
    field = pltpu.VMEM((rows, gauges, columns), F32)
    work = pltpu.VMEM(layers, F32)

    height, divergence, even_out, odd_out, courant_x, courant_y = pl.pallas_call(
        bind(load_kernel, rows),
        out_shape=(
            shaped(*layers), shaped(*layers), shaped(vectors, 8, columns), shaped(vectors, 8, columns),
            shaped(rows, columns), shaped(rows, columns),
        ),
        in_specs=[HBM] * 6,
        out_specs=(VMEM,) * 6,
        scratch_shapes=[field] * 3 + [pltpu.VMEM((rows, columns), jnp.int32), pltpu.SemaphoreType.DMA((7,))],
        compiler_params=params(LOAD_MIB),
        name="load",
    )(
        in_hbm(terminal_elevation.reshape(flat)),
        in_hbm(terminal_flux_x.reshape(flat)),
        in_hbm(terminal_flux_y.reshape(flat)),
        in_hbm(courant_x),
        in_hbm(courant_y),
        in_hbm(land_sea),
    )
    even_in = lax.ppermute(even_out, "gy", pairs("gy", 0))
    odd_in = lax.ppermute(odd_out, "gy", pairs("gy", 1))

    center_h, center_d, token = pl.pallas_call(
        bind(center_first_kernel, rows, ITERS // 2),
        out_shape=(shaped(*layers), shaped(*layers), shaped(8, columns)),
        in_specs=[VMEM] * 4,
        out_specs=(VMEM,) * 3,
        compiler_params=params(4),
        cost_estimate=pl.CostEstimate(flops=COST, bytes_accessed=2**20, transcendentals=0),
        name="center_first",
    )(height, divergence, courant_x, courant_y)

    x_even_out, x_odd_out = pl.pallas_call(
        bind(middle_kernel, rows),
        out_shape=(shaped(MESSAGE, 8, columns),) * 2,
        in_specs=[VMEM] * 9,
        out_specs=(VMEM,) * 2,
        compiler_params=params(4),
        name="middle",
    )(even_in, odd_in, even_out, odd_out, height, divergence, courant_x, courant_y, token)
    x_even_in = lax.ppermute(x_even_out, "gx", pairs("gx", 0))
    x_odd_in = lax.ppermute(x_odd_out, "gx", pairs("gx", 1))

    center = pl.pallas_call(
        bind(center_second_kernel, rows, ITERS - ITERS // 2),
        out_shape=shaped(*layers),
        in_specs=[VMEM] * 4,
        out_specs=VMEM,
        scratch_shapes=[field],
        compiler_params=params(4),
        cost_estimate=pl.CostEstimate(flops=COST, bytes_accessed=2**20, transcendentals=0),
        name="center_second",
    )(center_h, center_d, courant_x, courant_y)

    count = rows // 2 + W
    packed = (count + 8, gauges, columns)
    partial_out, bh0, bd0, cbx, cby, sums, homes = pl.pallas_call(
        bind(strips_kernel, rows),
        out_shape=(
            shaped(*flat), shaped(*packed), shaped(*packed), shaped(count, columns), shaped(count, columns),
            shaped(slots_x, 8, columns), shaped(slots, columns, dtype=jnp.int32),
        ),
        in_specs=[VMEM] * 11 + [SMEM] * 2,
        out_specs=(HBM,) + (VMEM,) * 6,
        scratch_shapes=[pltpu.VMEM(packed, F32), pltpu.VMEM(packed, F32), field]
        + [pltpu.VMEM((vectors, 8, columns), F32)] * 2
        + [pltpu.SemaphoreType.DMA],
        compiler_params=params(8),
        cost_estimate=pl.CostEstimate(flops=COST, bytes_accessed=2**20, transcendentals=0),
        name="strips",
    )(
        even_in, odd_in, even_out, odd_out, height, divergence, courant_x, courant_y, center,
        land_sea, uplift, tile_patches.reshape(-1), patch_home,
    )

    depth = 3 * W
    out, message = pl.pallas_call(
        bind(bands_kernel, rows),
        out_shape=(shaped(*flat), shaped(devices, columns)),
        in_specs=[VMEM] * 14 + [HBM],
        out_specs=(HBM, VMEM),
        input_output_aliases={14: 0},
        scratch_shapes=[
            pltpu.VMEM((3, depth, 8, columns), F32),
            pltpu.VMEM((3, depth, 8, columns), F32),
            pltpu.VMEM((3, depth, columns), F32),
            pltpu.VMEM((3, depth, columns), F32),
            pltpu.VMEM((2 * W, 8, columns), F32),
            pltpu.SemaphoreType.DMA,
        ],
        compiler_params=params(4),
        name="bands",
    )(
        x_even_in, x_odd_in, height, divergence, courant_x, courant_y, bh0, bd0, cbx, cby,
        land_sea, uplift, sums, homes, partial_out,
    )
    received = lax.all_to_all(message, ("gx", "gy"), 0, 0, tiled=True)
    gradient = pl.pallas_call(
        final_kernel,
        out_shape=shaped(patch_home.shape[0] // devices, gauges),
        in_specs=[VMEM],
        out_specs=VMEM,
        name="final",
    )(received)
    return (out.reshape(gauges, rows, columns), gradient)


LOAD_MIB = 8
COST = 40_000_000


def solution(mesh):
    in_specs = (
        P(None, "gx", "gy"),
        P(None, "gx", "gy"),
        P(None, "gx", "gy"),
        P("gx", "gy"),
        P("gx", "gy"),
        P("gx", "gy"),
        P("gx", "gy"),
        P(),
        P(),
    )
    out_specs = (P(None, "gx", "gy"), P(("gx", "gy"), None))
    return jax.shard_map(body, mesh=mesh, in_specs=in_specs, out_specs=out_specs, check_vma=False)
```

```python
import jax
import jax.numpy as jnp
from jax import lax
from jax.experimental import pallas as pl
from jax.experimental.pallas import tpu as pltpu
from jax.sharding import PartitionSpec as P

BS = 64
ITERS = 8
LANES = 128
W = 8
GROUPS = LANES // W
F32 = jnp.float32
VMEM = pl.BlockSpec(memory_space=pltpu.VMEM)
SMEM = pl.BlockSpec(memory_space=pltpu.SMEM)
HBM = pl.BlockSpec(memory_space=pl.ANY)


def lanes_of(shape=(8, LANES)):
    return lax.broadcasted_iota(jnp.int32, shape, len(shape) - 1)


def roll(vector, distance):
    distance = distance % LANES
    return pltpu.roll(vector, distance, vector.ndim - 1) if distance else vector


def params(mebibytes):
    return pltpu.CompilerParams(vmem_limit_bytes=mebibytes * 2**20)


def tile(ref, row):
    return ref[pl.ds(row if isinstance(row, int) else pl.multiple_of(row, 8), 8), :]


def payload_layout(rows):
    heights = rows // GROUPS
    tiles = rows // 8 // GROUPS
    return (0, heights, 2 * heights, 2 * heights + tiles, 2 * heights + 2 * tiles)


def advance(items, lag):
    live = {}
    written = {}
    for i in range(-2 * lag, len(items)):
        if i + 2 * lag < len(items):
            h_in, _, _, _, _, _, r, has_above, below = items[i + 2 * lag]
            assert written.get((id(h_in), r), -(10**9)) < i
            height = h_in[r]
            live[i + 2 * lag] = [
                height,
                roll(height, LANES - 1),
                h_in[r - 1] if has_above else None,
                h_in[r + 1] if below == "row" else None,
                None,
                None,
            ]
        if 0 <= i + lag < len(items):
            state = live[i + lag]
            coef_y, r = items[i + lag][5], items[i + lag][6]
            along = coef_y[pl.ds(r, 1), :] * (state[1] - state[0])
            state[4] = along
            state[5] = roll(along, 1)
        if i >= 0:
            h_in, d_in, h_out, d_out, coef_x, _, r, has_above, below = items[i]
            height, _, above, under, along, along_before = live.pop(i)
            if below == "item":
                under = live[i + 1][0]
            if has_above:
                before = coef_x[pl.ds(r - 1, 1), :] * (height - above)
            elif i == 0 or items[i - 1][8] != "item":
                before = None
            flux = coef_x[pl.ds(r, 1), :] * ((under - height) if under is not None else -height)
            change = along - along_before + (flux if before is None else flux - before)
            divergence = d_in[r] + change
            d_out[r] = divergence
            h_out[r] = height + divergence
            written[(id(h_out), r)] = i
            before = flux


class Stores:
    def __init__(self, lag):
        self.lag, self.waiting = lag, []

    def __call__(self, ref, place, value):
        self.waiting.append((ref, place, value))
        if len(self.waiting) > self.lag:
            self.release(1)

    def release(self, count=None):
        for ref, place, value in self.waiting[:count]:
            ref[place] = value
        self.waiting = self.waiting[count:] if count else []


def rows_of(count, refs):
    return [refs + (r, False, "item" if r + 1 < count else None) for r in range(count)]


def run_steps(count, steps, unroll, first, then, lag):
    if first is not None:
        head = rows_of(count, first)
        for _ in range(unroll - 1):
            head = head + rows_of(count, then)
        advance(head, lag)

    def again(t, carry):
        advance(rows_of(count, then) * unroll, lag)
        return carry

    rounds = steps // unroll - (first is not None)
    if rounds == 1:
        again(0, 0)
    elif rounds:
        lax.fori_loop(0, rounds, again, 0)


def load_kernel(
    rows, h_hbm, x_hbm, y_hbm, cx_hbm, cy_hbm, wet_hbm,
    h_out, d_out, even_out, odd_out, cx_ref, cy_ref, hb, xb, yb, wet_ref, sems,
):
    gauges = 8
    parts = 4
    size = rows // parts
    plain = [
        pltpu.make_async_copy(source, target, sems.at[parts + i])
        for i, (source, target) in enumerate(((cx_hbm, cx_ref), (cy_hbm, cy_ref), (wet_hbm, wet_ref)))
    ]
    for copy in plain:
        copy.start()
    for part in range(parts):
        for source, target in ((y_hbm, yb), (x_hbm, xb), (h_hbm, hb)):
            for gauge in range(gauges):
                pltpu.make_async_copy(
                    source.at[pl.ds(gauge * rows + part * size, size)],
                    target.at[pl.ds(part * size, size), gauge],
                    sems.at[part],
                ).start()

    even = lax.rem(lax.axis_index("gy"), 2) == 0
    lane = lanes_of()
    group = lane // W
    at_h, at_d, at_cx, at_cy, at_g = payload_layout(rows)

    def put(place, to_left, to_right):
        even_out[place] = jnp.where(even, to_right, to_left)
        odd_out[place] = jnp.where(even, to_left, to_right)

    for copy in plain:
        copy.wait()
    for ref, place in ((cx_ref, at_cx), (cy_ref, at_cy)):
        for p in range(rows // 8 // GROUPS):
            to_left = to_right = jnp.zeros((8, LANES), F32)
            for k in range(GROUPS):
                value = ref[pl.ds((p * GROUPS + k) * 8, 8), :]
                to_left = jnp.where(group == k, roll(value, W * k), to_left)
                to_right = jnp.where(group == k, roll(value, W * k + W), to_right)
            put(place + p, to_left, to_right)

    state = {}

    def early(r):
        along_y = cy_ref[pl.ds(r, 1), :] * yb[r]
        state[r] = (along_y, roll(along_y, 1))

    def late(r, above, sides):
        along_y, before_y = state.pop(r)
        along_x = cx_ref[pl.ds(r, 1), :] * xb[r]
        height = wet_ref[pl.ds(r, 1), :].astype(F32) * hb[r]
        part = along_y + along_x if above is None else along_y + (along_x - above)
        divergence = part - jnp.where(lane == 0, 0.0, before_y)
        outgoing = jnp.where(lane == 0, -before_y, divergence)
        h_out[r] = height
        d_out[r] = divergence
        k = r % GROUPS
        mine = group == k
        new = (
            roll(height, W * k),
            roll(divergence, W * k),
            roll(height, W * k + W),
            roll(outgoing, W * k + W - 1),
        )
        sides = new if k == 0 else tuple(jnp.where(mine, n, s) for n, s in zip(new, sides))
        if k == GROUPS - 1:
            put(at_h + r // GROUPS, sides[0], sides[2])
            put(at_d + r // GROUPS, sides[1], sides[3])
        return along_x, sides

    above, sides = None, None
    lag = 16
    for part in range(parts):
        done = hb.at[pl.ds(0, 3 * size)]
        pltpu.make_async_copy(done, done, sems.at[part]).wait()
        low, high = part * size, (part + 1) * size
        for r in range(low - lag, high):
            if r + lag < high:
                early(r + lag)
            if r >= low:
                above, sides = late(r, above, sides)
    d_out[rows] = -above
    put(at_g, -above, roll(-above, W))


def center_first_kernel(rows, steps, h_ref, d_ref, cx_ref, cy_ref, h_out, d_out, token):
    first = (h_ref, d_ref, h_out, d_out, cx_ref, cy_ref)
    then = (h_out, d_out, h_out, d_out, cx_ref, cy_ref)
    run_steps(rows, steps, 2, first, then, 24)
    token[...] = jnp.zeros((8, LANES), F32)


def center_second_kernel(rows, steps, h_in, d_in, cx_ref, cy_ref, h_out, d_out):
    then = (h_out, d_out, h_out, d_out, cx_ref, cy_ref)
    run_steps(rows, steps, 2, None, then, 24)


SECOND = 32


def strip(lane, own, from_left, from_right, shift=0):
    at = (lane - shift) % LANES
    return jnp.where(
        at >= LANES - 2 * W,
        roll(own, shift),
        jnp.where(at < W, from_right, jnp.where(at < 64, from_left, roll(own, 64 + shift))),
    )


def strip_divergence(lane, own, from_left, from_right, shift=0):
    at = (lane - shift) % LANES
    middle = jnp.where(at >= 64, roll(own, 64 + shift), 0.0) + jnp.where(
        (at > 64 - W) & (at <= 64), from_left, 0.0
    )
    return jnp.where(at >= LANES - 2 * W, roll(own, shift), jnp.where(at < W, from_right, middle))


def second_lanes(lane):
    return ((lane >= 16) & (lane < 40)) | ((lane >= 88) & (lane < 112))


def merge(lane, center, packed, lower):
    shift = SECOND if lower else 0
    left, right = roll(packed, 64 - shift), roll(packed, -shift)
    return jnp.where(lane < W, left, jnp.where(lane >= LANES - W, right, center))


class Sides:
    def __init__(self, even_in, odd_in, even_out, odd_out):
        self.even = lax.rem(lax.axis_index("gy"), 2) == 0
        self.lane = lanes_of()
        self.refs = (even_in, odd_in, even_out, odd_out)

    def left(self, place):
        even_in, odd_in, _, _ = self.refs
        return jnp.where(self.even, odd_in[place], even_in[place])

    def right(self, place):
        even_in, odd_in, _, _ = self.refs
        return jnp.where(self.even, even_in[place], odd_in[place])

    def right_divergence(self, place):
        _, _, even_out, odd_out = self.refs
        sent = jnp.where(self.even, even_out[place], odd_out[place])
        return self.right(place) + jnp.where(self.lane % W == 0, roll(sent, -(W - 1)), 0.0)


def middle_kernel(rows, even_in, odd_in, even_out, odd_out, h_ref, d_ref, cx_ref, cy_ref, token, x_even, x_odd):
    side = Sides(even_in, odd_in, even_out, odd_out)
    lane, group = side.lane, side.lane // W
    at_h, at_d, at_cx, at_cy, at_g = payload_layout(rows)
    last_h, last_c = rows // GROUPS - 1, rows // 8 // GROUPS - 1
    even = lax.rem(lax.axis_index("gx"), 2) == 0
    store = Stores(24)

    def put(place, up, down):
        store(x_even, place, jnp.where(even, down, up))
        store(x_odd, place, jnp.where(even, up, down))

    for j in range(W):
        put(j, h_ref[j], h_ref[rows - W + j])
        put(W + j, d_ref[j], d_ref[rows - W + j])
    first = lane < 64
    put(
        2 * W,
        jnp.where(first, side.left(at_h), roll(side.right(at_h), 64)),
        jnp.where(first, roll(side.left(at_h + last_h), 64), side.right(at_h + last_h)),
    )
    put(
        2 * W + 1,
        jnp.where(first, side.left(at_d), roll(side.right_divergence(at_d), 64)),
        jnp.where(first, roll(side.left(at_d + last_h), 64), side.right_divergence(at_d + last_h)),
    )
    put(2 * W + 2, cx_ref[0:8, :], cx_ref[rows - 8 : rows, :])
    put(2 * W + 3, cy_ref[0:8, :], cy_ref[rows - 8 : rows, :])

    def gathered(pieces):
        result = pieces[0]
        for k, piece in enumerate(pieces[1:], 1):
            result = jnp.where(group == k, roll(piece, W * k), result)
        return result

    g_left, g_right = side.left(at_g), side.right(at_g)
    put(
        2 * W + 4,
        gathered([side.left(at_cx), side.right(at_cx), side.left(at_cy), side.right(at_cy), g_left, g_right]),
        gathered(
            [roll(side.left(at_cx + last_c), W), roll(side.right(at_cx + last_c), W)]
            + [roll(side.left(at_cy + last_c), W), roll(side.right(at_cy + last_c), W)]
            + [g_left, g_right]
        ),
    )
    put(2 * W + 5, d_ref[rows], d_ref[rows])
    store.release()


MESSAGE = 2 * W + 6


def strips_kernel(
    rows, even_in, odd_in, even_out, odd_out, h_ref, d_ref, cx_ref, cy_ref, done_ref, wet_ref, uplift_ref, lists_ref, home_ref,
    merged, bh0, bd0, cbx, cby, sums, homes, hb, db, lefts, rights,
):
    side = Sides(even_in, odd_in, even_out, odd_out)
    lane = side.lane
    second = second_lanes(lane)
    at_h, at_d, at_cx, at_cy, at_g = payload_layout(rows)
    count = rows // 2 + W
    offset = rows // 2 - W
    store = Stores(24)
    for place in range(at_g + 1):
        store(lefts, place, side.left(place))
        right = side.right_divergence(place) if at_d <= place < at_cx else side.right(place)
        store(rights, place, right)
    store.release()

    for ref, target, place in ((cx_ref, cbx, at_cx), (cy_ref, cby, at_cy)):

        def strip_tile(row, shift):
            p, k = divmod(row // 8, GROUPS)
            left = roll(lefts[place + p], 64 - W - W * k + shift)
            right = roll(rights[place + p], shift - W * k)
            return strip(lane, ref[pl.ds(row, 8), :], left, right, shift)

        for row in range(0, count, 8):
            value = jnp.where(second, strip_tile(row + offset, SECOND), strip_tile(row, 0))
            store(target, pl.ds(row, 8), value)

    def strips_at(row, m, k, shift):
        left, right = lefts[at_h + m], rights[at_h + m]
        left, right = roll(left, 64 - W - W * k + shift), roll(right, shift - W * k)
        height = strip(lane, h_ref[row], left, right, shift)
        left, right = lefts[at_d + m], rights[at_d + m]
        left, right = roll(left, 64 - W + 1 - W * k + shift), roll(right, shift - W * k)
        return height, strip_divergence(lane, d_ref[row], left, right, shift)

    def build(b, length):
        values = []
        for k in range(length):
            row = b * GROUPS + k
            upper = strips_at(row, b, k, 0)
            lower_m, lower_k = divmod(offset + k, GROUPS)
            lower = strips_at(row + offset, b + lower_m, lower_k, SECOND)
            values.append([jnp.where(second, low, up) for up, low in zip(upper, lower)])
        for k in range(length):
            bh0[b * GROUPS + k], bd0[b * GROUPS + k] = values[k]
        return length

    lax.fori_loop(0, count // GROUPS, lambda b, carry: build(b, GROUPS) and carry, 0)
    if count % GROUPS:
        build(count // GROUPS, count % GROUPS)
    store.release()
    bd0[count] = strip(lane, d_ref[rows], roll(lefts[at_g], 64 - W), rights[at_g])
    first = (bh0, bd0, hb, db, cbx, cby)
    then = (hb, db, hb, db, cbx, cby)
    run_steps(count, ITERS, 2, first, then, 24)

    bounds = slot_bounds(rows)
    for u in range(len(bounds) - 1):
        total = jnp.zeros((8, LANES), F32)
        for r in range(max(bounds[u], W), min(bounds[u + 1], rows - W)):
            lower = r >= rows // 2
            value = merge(lane, done_ref[r], hb[r - offset if lower else r], lower)
            store(merged, r, value)
            weight = wet_ref[pl.ds(r, 1), :].astype(F32) * uplift_ref[pl.ds(r, 1), :] * (1.0 / BS)
            total = total + weight * value
        store(sums, u, total)
    store.release()
    tile_row, tile_column = lax.axis_index("gx"), lax.axis_index("gy")
    slots = homes.shape[0]
    for s in range(slots):
        patch = lists_ref[tile_row, tile_column, s]
        homes[pl.ds(s, 1), :] = jnp.full((1, LANES), home_ref[patch], jnp.int32)


def slot_bounds(length):
    return [0] + list(range(BS // 2, length, BS)) + [length]


def bands_kernel(
    rows, x_even_in, x_odd_in, h_ref, d_ref, cx_ref, cy_ref, bh0, bd0, cbx, cby, done_wet, uplift_ref, sums_ref, homes_ref, merged,
    out_hbm, message, hs, ds, cxs, cys, edge, sems,
):
    inner = rows - 2 * W
    copies = [
        pltpu.make_async_copy(
            merged.at[pl.ds(W, inner), g], out_hbm.at[pl.ds(g * rows + W, inner)], sems.at[g]
        )
        for g in range(8)
    ]
    for copy in copies:
        copy.start()
    lane = lanes_of()
    second = second_lanes(lane)
    even = lax.rem(lax.axis_index("gx"), 2) == 0
    depth = 3 * W
    count = rows // 2 + W

    def above(place):
        return jnp.where(even, x_odd_in[place], x_even_in[place])

    def below(place):
        return jnp.where(even, x_even_in[place], x_odd_in[place])

    def both(upper, lower):
        return jnp.where(second, lower, upper)

    store = Stores(24)

    top, bottom, strips = 0, 1, 2
    for c, (ref, mine, packed) in enumerate(((cxs, cx_ref, cbx), (cys, cy_ref, cby))):
        halos = []
        for got in (above, below):
            value, corner = got(2 * W + 2 + c), got(2 * W + 4)
            halos.append(
                (
                    value,
                    strip(
                        lane, value, roll(corner, 64 - W - 2 * W * c), roll(corner, -W - 2 * W * c)
                    ),
                )
            )
        store(ref, (top, slice(0, W)), halos[0][0])
        store(ref, (top, slice(W, depth)), mine[0 : 2 * W, :])
        store(ref, (bottom, slice(0, 2 * W)), mine[rows - 2 * W : rows, :])
        store(ref, (bottom, slice(2 * W, depth)), halos[1][0])
        store(ref, (strips, slice(0, W)), both(halos[0][1], packed[count - 2 * W : count - W, :]))
        store(ref, (strips, slice(W, 2 * W)), both(packed[0:W, :], packed[count - W : count, :]))
        store(
            ref, (strips, slice(2 * W, depth)), both(packed[W : 2 * W, :], roll(halos[1][1], SECOND))
        )

    def halo_strips(got, j):
        packed_h, packed_d = got(2 * W), got(2 * W + 1)
        return (
            strip(lane, got(j), roll(packed_h, 64 - W - W * j), roll(packed_h, -64 - W * j)),
            strip_divergence(
                lane, got(W + j), roll(packed_d, 64 - W + 1 - W * j), roll(packed_d, -64 - W * j)
            ),
        )

    flux, corner = above(2 * W + 5), above(2 * W + 4)
    flux_strip = strip(lane, flux, roll(corner, 64 - W - 4 * W), roll(corner, -5 * W))
    for j in range(W):
        upper, lower = halo_strips(above, j), halo_strips(below, j)
        h_last, d_last = roll(lower[0], SECOND), roll(lower[1], SECOND)
        d_first, d_below = bd0[j], below(W + j)
        d_top = d_ref[j]
        if j == 0:
            d_first = d_first + flux_strip
            d_top = d_top + flux
            d_below = d_below + d_ref[rows]
            d_last = d_last + roll(bd0[count], SECOND)
        low, packed_low = rows - 2 * W + j, count - 2 * W + j
        for band, place, height, divergence in (
            (top, j, above(j), above(W + j)),
            (top, W + j, h_ref[j], d_top),
            (top, 2 * W + j, h_ref[W + j], d_ref[W + j]),
            (bottom, j, h_ref[low], d_ref[low]),
            (bottom, W + j, h_ref[low + W], d_ref[low + W]),
            (bottom, 2 * W + j, below(j), d_below),
            (strips, j, both(upper[0], bh0[packed_low]), both(upper[1], bd0[packed_low])),
            (strips, W + j, both(bh0[j], bh0[packed_low + W]), both(d_first, bd0[packed_low + W])),
            (strips, 2 * W + j, both(bh0[W + j], h_last), both(bd0[W + j], d_last)),
        ):
            store(hs, (band, place), height)
            store(ds, (band, place), divergence)
    store.release()

    views = [(hs.at[b], ds.at[b], hs.at[b], ds.at[b], cxs.at[b], cys.at[b]) for b in range(3)]
    items = []
    for t in range(1, ITERS + 1):
        low, high = t, depth - t
        for view in views:
            for r in range(low, high):
                items.append(view + (r, r == low, "item" if r + 1 < high else "row"))
    advance(items, 8)

    bounds = slot_bounds(rows)
    slots_x = len(bounds) - 1
    totals = [sums_ref[u] for u in range(slots_x)]
    for band, first in ((top, 0), (bottom, rows - W)):
        slot = 0 if band == top else slots_x - 1
        for j in range(W):
            value = merge(lane, hs[band, W + j], hs[strips, W + j], band == bottom)
            store(edge, band * W + j, value)
            weight = done_wet[pl.ds(first + j, 1), :].astype(F32) * uplift_ref[pl.ds(first + j, 1), :] * (1.0 / BS)
            totals[slot] = totals[slot] + weight * value
    store.release()
    edges = [
        pltpu.make_async_copy(
            edge.at[pl.ds(band * W, W), g],
            out_hbm.at[pl.ds(g * rows + first, W)],
            sems.at[8 + 8 * band + g],
        )
        for band, first in ((0, 0), (1, rows - W))
        for g in range(8)
    ]
    for copy in edges:
        copy.start()

    column_bounds = slot_bounds(LANES)
    slots_y = len(column_bounds) - 1
    devices = message.shape[0]
    gauge = lax.broadcasted_iota(jnp.int32, (8, LANES), 0)
    shape = (devices, LANES)
    here = lanes_of(shape)
    per_device = 8
    home_of = jnp.where(
        here < per_device * 8,
        lax.broadcasted_iota(jnp.int32, shape, 0) * per_device + here // 8,
        -1,
    )
    built = jnp.zeros(shape, F32)
    for u in range(slots_x):
        for w in range(slots_y):
            inside = (lane >= column_bounds[w]) & (lane < column_bounds[w + 1])
            total = jnp.sum(jnp.where(inside, totals[u], 0.0), axis=1, keepdims=True)
            spread = jnp.sum(jnp.where(lane % 8 == gauge, total, 0.0), axis=0, keepdims=True)
            home = homes_ref[pl.ds(u * slots_y + w, 1), :]
            built = built + jnp.where(home_of == home, spread, 0.0)
    message[...] = built
    for copy in copies + edges:
        copy.wait()


def final_kernel(received, gradient):
    total = jnp.sum(received[...], axis=0, keepdims=True)
    lane = lanes_of()
    row = lax.broadcasted_iota(jnp.int32, (8, LANES), 0)
    result = jnp.zeros((8, LANES), F32)
    for k in range(8):
        result = jnp.where(row == k, roll(jnp.broadcast_to(total, (8, LANES)), -8 * k), result)
    gradient[...] = result[:, :8]


def pairs(axis, first):
    return [
        pair
        for i in range(first, lax.axis_size(axis) - 1, 2)
        for pair in ((i, i + 1), (i + 1, i))
    ]


def in_vmem(*arrays):
    return [pltpu.with_memory_space_constraint(array, pltpu.VMEM) for array in arrays]


def in_hbm(array):
    return pltpu.with_memory_space_constraint(array, pltpu.HBM)


def shaped(*shape, dtype=F32):
    return jax.ShapeDtypeStruct(shape, dtype)


def bind(kernel, *sizes):
    def bound(*refs):
        kernel(*sizes, *refs)

    return bound


def body(
    terminal_elevation,
    terminal_flux_x,
    terminal_flux_y,
    courant_x,
    courant_y,
    land_sea,
    uplift,
    tile_patches,
    patch_home,
):
    gauges, rows, columns = terminal_elevation.shape
    flat = (gauges * rows, columns)
    layers = (rows + 8, gauges, columns)
    devices = lax.axis_size("gx") * lax.axis_size("gy")
    slots = tile_patches.shape[2]
    slots_x = len(slot_bounds(rows)) - 1
    vectors = payload_layout(rows)[-1] + 1
    field = pltpu.VMEM((rows, gauges, columns), F32)
    work = pltpu.VMEM(layers, F32)

    height, divergence, even_out, odd_out, courant_x, courant_y = pl.pallas_call(
        bind(load_kernel, rows),
        out_shape=(
            shaped(*layers), shaped(*layers), shaped(vectors, 8, columns), shaped(vectors, 8, columns),
            shaped(rows, columns), shaped(rows, columns),
        ),
        in_specs=[HBM] * 6,
        out_specs=(VMEM,) * 6,
        scratch_shapes=[field] * 3 + [pltpu.VMEM((rows, columns), jnp.int32), pltpu.SemaphoreType.DMA((7,))],
        compiler_params=params(LOAD_MIB),
        name="load",
    )(
        in_hbm(terminal_elevation.reshape(flat)),
        in_hbm(terminal_flux_x.reshape(flat)),
        in_hbm(terminal_flux_y.reshape(flat)),
        in_hbm(courant_x),
        in_hbm(courant_y),
        in_hbm(land_sea),
    )
    even_in = lax.ppermute(even_out, "gy", pairs("gy", 0))
    odd_in = lax.ppermute(odd_out, "gy", pairs("gy", 1))

    center_h, center_d, token = pl.pallas_call(
        bind(center_first_kernel, rows, ITERS // 2),
        out_shape=(shaped(*layers), shaped(*layers), shaped(8, columns)),
        in_specs=[VMEM] * 4,
        out_specs=(VMEM,) * 3,
        compiler_params=params(2),
        cost_estimate=pl.CostEstimate(flops=COST, bytes_accessed=2**20, transcendentals=0),
        name="center_first",
    )(*in_vmem(height, divergence, courant_x, courant_y))

    x_even_out, x_odd_out = pl.pallas_call(
        bind(middle_kernel, rows),
        out_shape=(shaped(MESSAGE, 8, columns),) * 2,
        in_specs=[VMEM] * 9,
        out_specs=(VMEM,) * 2,
        compiler_params=params(2),
        name="middle",
    )(*in_vmem(even_in, odd_in, even_out, odd_out, height, divergence, courant_x, courant_y, token))
    x_even_in = lax.ppermute(x_even_out, "gx", pairs("gx", 0))
    x_odd_in = lax.ppermute(x_odd_out, "gx", pairs("gx", 1))

    center, _ = pl.pallas_call(
        bind(center_second_kernel, rows, ITERS - ITERS // 2),
        out_shape=(shaped(*layers),) * 2,
        in_specs=[VMEM] * 4,
        out_specs=(VMEM,) * 2,
        input_output_aliases={0: 0, 1: 1},
        compiler_params=params(2),
        cost_estimate=pl.CostEstimate(flops=COST, bytes_accessed=2**20, transcendentals=0),
        name="center_second",
    )(*in_vmem(center_h, center_d, courant_x, courant_y))

    count = rows // 2 + W
    packed = (count + 8, gauges, columns)
    merged, bh0, bd0, cbx, cby, sums, homes = pl.pallas_call(
        bind(strips_kernel, rows),
        out_shape=(
            shaped(rows, gauges, columns), shaped(*packed), shaped(*packed), shaped(count, columns), shaped(count, columns),
            shaped(slots_x, 8, columns), shaped(slots, columns, dtype=jnp.int32),
        ),
        in_specs=[VMEM] * 11 + [SMEM] * 2,
        out_specs=(VMEM,) * 7,
        scratch_shapes=[pltpu.VMEM(packed, F32)] * 2 + [pltpu.VMEM((vectors, 8, columns), F32)] * 2,
        compiler_params=params(5),
        cost_estimate=pl.CostEstimate(flops=COST, bytes_accessed=2**20, transcendentals=0),
        name="strips",
    )(
        *in_vmem(even_in, odd_in, even_out, odd_out, height, divergence, courant_x, courant_y, center),
        land_sea, uplift, tile_patches, patch_home,
    )

    depth = 3 * W
    out, message = pl.pallas_call(
        bind(bands_kernel, rows),
        out_shape=(shaped(*flat), shaped(devices, columns)),
        in_specs=[VMEM] * 15,
        out_specs=(HBM, VMEM),
        scratch_shapes=[
            pltpu.VMEM((3, depth, 8, columns), F32),
            pltpu.VMEM((3, depth, 8, columns), F32),
            pltpu.VMEM((3, depth, columns), F32),
            pltpu.VMEM((3, depth, columns), F32),
            pltpu.VMEM((2 * W, 8, columns), F32),
            pltpu.SemaphoreType.DMA((24,)),
        ],
        compiler_params=params(2),
        name="bands",
    )(
        *in_vmem(x_even_in, x_odd_in, height, divergence, courant_x, courant_y, bh0, bd0, cbx, cby),
        land_sea, uplift, *in_vmem(sums, homes, merged),
    )
    received = lax.all_to_all(message, ("gx", "gy"), 0, 0, tiled=True)
    gradient = pl.pallas_call(
        final_kernel,
        out_shape=shaped(patch_home.shape[0] // devices, gauges),
        in_specs=[VMEM],
        out_specs=VMEM,
        name="final",
    )(received)
    return (out.reshape(gauges, rows, columns), gradient)


LOAD_MIB = 6
COST = 40_000_000


def solution(mesh):
    in_specs = (
        P(None, "gx", "gy"),
        P(None, "gx", "gy"),
        P(None, "gx", "gy"),
        P("gx", "gy"),
        P("gx", "gy"),
        P("gx", "gy"),
        P("gx", "gy"),
        P(),
        P(),
    )
    out_specs = (P(None, "gx", "gy"), P(("gx", "gy"), None))
    return jax.shard_map(body, mesh=mesh, in_specs=in_specs, out_specs=out_specs, check_vma=False)
```

```python
import jax
import jax.numpy as jnp
from jax import lax
from jax.experimental import pallas as pl
from jax.experimental.pallas import tpu as pltpu
from jax.sharding import PartitionSpec as P

BS = 64
ITERS = 8
LANES = 128
W = 8
GROUPS = LANES // W
F32 = jnp.float32
VMEM = pl.BlockSpec(memory_space=pltpu.VMEM)
HBM = pl.BlockSpec(memory_space=pl.ANY)


def lanes_of(shape=(8, LANES)):
    return lax.broadcasted_iota(jnp.int32, shape, len(shape) - 1)


def roll(vector, distance):
    distance = distance % LANES
    return pltpu.roll(vector, distance, vector.ndim - 1) if distance else vector


def params(mebibytes):
    return pltpu.CompilerParams(vmem_limit_bytes=mebibytes * 2**20)


def tile(ref, row):
    return ref[pl.ds(row if isinstance(row, int) else pl.multiple_of(row, 8), 8), :]


def payload_layout(rows):
    heights = rows // GROUPS
    tiles = rows // 8 // GROUPS
    return (0, heights, 2 * heights, 2 * heights + tiles, 2 * heights + 2 * tiles)


def advance(items, lag):
    live = {}
    written = {}
    for i in range(-2 * lag, len(items)):
        if i + 2 * lag < len(items):
            h_in, _, _, _, _, _, r, has_above, below = items[i + 2 * lag]
            assert written.get((id(h_in), r), -(10**9)) < i
            height = h_in[r]
            live[i + 2 * lag] = [
                height,
                roll(height, LANES - 1),
                h_in[r - 1] if has_above else None,
                h_in[r + 1] if below == "row" else None,
                None,
                None,
            ]
        if 0 <= i + lag < len(items):
            state = live[i + lag]
            coef_y, r = items[i + lag][5], items[i + lag][6]
            along = coef_y[pl.ds(r, 1), :] * (state[1] - state[0])
            state[4] = along
            state[5] = roll(along, 1)
        if i >= 0:
            h_in, d_in, h_out, d_out, coef_x, _, r, has_above, below = items[i]
            height, _, above, under, along, along_before = live.pop(i)
            if below == "item":
                under = live[i + 1][0]
            if has_above:
                before = coef_x[pl.ds(r - 1, 1), :] * (height - above)
            elif i == 0 or items[i - 1][8] != "item":
                before = None
            flux = coef_x[pl.ds(r, 1), :] * ((under - height) if under is not None else -height)
            change = along - along_before + (flux if before is None else flux - before)
            divergence = d_in[r] + change
            d_out[r] = divergence
            h_out[r] = height + divergence
            written[(id(h_out), r)] = i
            before = flux


class Stores:
    def __init__(self, lag):
        self.lag, self.waiting = lag, []

    def __call__(self, ref, place, value):
        self.waiting.append((ref, place, value))
        if len(self.waiting) > self.lag:
            self.release(1)

    def release(self, count=None):
        for ref, place, value in self.waiting[:count]:
            ref[place] = value
        self.waiting = self.waiting[count:] if count else []


def run_steps(count, steps, first, then, lag):
    items = []
    for t in steps:
        refs = first if t == steps[0] else then
        for r in range(t, count - t):
            items.append(refs + (r, t > 0, "item" if r + 1 < count - t else "row" if t else None))
    advance(items, lag)


def load_kernel(
    rows, h_hbm, x_hbm, y_hbm, cx_hbm, cy_hbm, wet_hbm, lists_hbm, home_hbm,
    h_out, d_out, odd_out, even_out, cx_ref, cy_ref, homes, hb, xb, yb, wet_ref, lists_ref, home_ref, sems,
):
    gauges = 8
    parts = 4
    size = rows // parts
    plain = [
        pltpu.make_async_copy(source, target, sems.at[parts + i])
        for i, (source, target) in enumerate(((cx_hbm, cx_ref), (cy_hbm, cy_ref), (wet_hbm, wet_ref)))
    ]
    scalars = [
        pltpu.make_async_copy(lists_hbm, lists_ref, sems.at[parts + 3]),
        pltpu.make_async_copy(home_hbm, home_ref, sems.at[parts + 4]),
    ]
    for copy in plain + scalars:
        copy.start()
    for part in range(parts):
        for source, target in ((y_hbm, yb), (x_hbm, xb), (h_hbm, hb)):
            for gauge in range(gauges):
                pltpu.make_async_copy(
                    source.at[pl.ds(gauge * rows + part * size, size)],
                    target.at[pl.ds(part * size, size), gauge],
                    sems.at[part],
                ).start()

    even = lax.rem(lax.axis_index("gy"), 2) == 0
    lane = lanes_of()
    group = lane // W
    at_h, at_d, at_cx, at_cy, at_g = payload_layout(rows)

    def put(place, to_left, to_right):
        even_out[place] = jnp.where(even, to_right, to_left)
        odd_out[place] = jnp.where(even, to_left, to_right)

    for copy in plain:
        copy.wait()
    for ref, place in ((cx_ref, at_cx), (cy_ref, at_cy)):
        for p in range(rows // 8 // GROUPS):
            to_left = to_right = jnp.zeros((8, LANES), F32)
            for k in range(GROUPS):
                value = ref[pl.ds((p * GROUPS + k) * 8, 8), :]
                to_left = jnp.where(group == k, roll(value, W * k), to_left)
                to_right = jnp.where(group == k, roll(value, W * k + W), to_right)
            put(place + p, to_left, to_right)

    state = {}

    def early(r):
        along_y = cy_ref[pl.ds(r, 1), :] * yb[r]
        state[r] = (along_y, roll(along_y, 1))

    def late(r, above, sides):
        along_y, before_y = state.pop(r)
        along_x = cx_ref[pl.ds(r, 1), :] * xb[r]
        height = wet_ref[pl.ds(r, 1), :].astype(F32) * hb[r]
        part = along_y + along_x if above is None else along_y + (along_x - above)
        divergence = part - jnp.where(lane == 0, 0.0, before_y)
        outgoing = jnp.where(lane == 0, -before_y, divergence)
        h_out[r] = height
        d_out[r] = divergence
        k = r % GROUPS
        mine = group == k
        new = (
            roll(height, W * k),
            roll(divergence, W * k),
            roll(height, W * k + W),
            roll(outgoing, W * k + W - 1),
        )
        sides = new if k == 0 else tuple(jnp.where(mine, n, s) for n, s in zip(new, sides))
        if k == GROUPS - 1:
            put(at_h + r // GROUPS, sides[0], sides[2])
            put(at_d + r // GROUPS, sides[1], sides[3])
        return along_x, sides

    above, sides = None, None
    lag = 16
    for part in range(parts):
        done = hb.at[pl.ds(0, 3 * size)]
        pltpu.make_async_copy(done, done, sems.at[part]).wait()
        low, high = part * size, (part + 1) * size
        for r in range(low - lag, high):
            if r + lag < high:
                early(r + lag)
            if r >= low:
                above, sides = late(r, above, sides)
    d_out[rows] = -above
    put(at_g, -above, roll(-above, W))

    for copy in scalars:
        copy.wait()
    tile_row, tile_column = lax.axis_index("gx"), lax.axis_index("gy")
    for slot in range(homes.shape[0]):
        patch = lists_ref[tile_row, tile_column, slot]
        homes[pl.ds(slot, 1), :] = jnp.full((1, LANES), home_ref[patch], jnp.int32)


def center_first_kernel(rows, steps, h_ref, d_ref, cx_ref, cy_ref, h_out, d_out, token):
    first = (h_ref, d_ref, h_out, d_out, cx_ref, cy_ref)
    then = (h_out, d_out, h_out, d_out, cx_ref, cy_ref)
    run_steps(rows, steps, first, then, 32)
    token[...] = jnp.zeros((8, LANES), F32)


def center_second_kernel(rows, steps, h_in, d_in, cx_ref, cy_ref, h_out, d_out):
    then = (h_out, d_out, h_out, d_out, cx_ref, cy_ref)
    run_steps(rows, steps, then, then, 32)


SECOND = 32


def strip(lane, own, from_left, from_right, shift=0):
    at = (lane - shift) % LANES
    return jnp.where(
        at >= LANES - 2 * W,
        roll(own, shift),
        jnp.where(at < W, from_right, jnp.where(at < 64, from_left, roll(own, 64 + shift))),
    )


def strip_divergence(lane, own, from_left, from_right, shift=0):
    at = (lane - shift) % LANES
    middle = jnp.where(at >= 64, roll(own, 64 + shift), 0.0) + jnp.where(
        (at > 64 - W) & (at <= 64), from_left, 0.0
    )
    return jnp.where(at >= LANES - 2 * W, roll(own, shift), jnp.where(at < W, from_right, middle))


def second_lanes(lane):
    return ((lane >= 16) & (lane < 40)) | ((lane >= 88) & (lane < 112))


def merge(lane, center, packed, lower):
    shift = SECOND if lower else 0
    left, right = roll(packed, 64 - shift), roll(packed, -shift)
    return jnp.where(lane < W, left, jnp.where(lane >= LANES - W, right, center))


class Sides:
    def __init__(self, even_in, odd_in, even_out, odd_out):
        self.even = lax.rem(lax.axis_index("gy"), 2) == 0
        self.lane = lanes_of()
        self.refs = (even_in, odd_in, even_out, odd_out)

    def left(self, place):
        even_in, odd_in, _, _ = self.refs
        return jnp.where(self.even, odd_in[place], even_in[place])

    def right(self, place):
        even_in, odd_in, _, _ = self.refs
        return jnp.where(self.even, even_in[place], odd_in[place])

    def right_divergence(self, place):
        _, _, even_out, odd_out = self.refs
        sent = jnp.where(self.even, even_out[place], odd_out[place])
        return self.right(place) + jnp.where(self.lane % W == 0, roll(sent, -(W - 1)), 0.0)


def middle_kernel(rows, even_in, odd_in, even_out, odd_out, h_ref, d_ref, cx_ref, cy_ref, token, x_even, x_odd):
    side = Sides(even_in, odd_in, even_out, odd_out)
    lane, group = side.lane, side.lane // W
    at_h, at_d, at_cx, at_cy, at_g = payload_layout(rows)
    last_h, last_c = rows // GROUPS - 1, rows // 8 // GROUPS - 1
    even = lax.rem(lax.axis_index("gx"), 2) == 0
    store = Stores(24)

    def put(place, up, down):
        store(x_even, place, jnp.where(even, down, up))
        store(x_odd, place, jnp.where(even, up, down))

    for j in range(W):
        put(j, h_ref[j], h_ref[rows - W + j])
        put(W + j, d_ref[j], d_ref[rows - W + j])
    first = lane < 64
    put(
        2 * W,
        jnp.where(first, side.left(at_h), roll(side.right(at_h), 64)),
        jnp.where(first, roll(side.left(at_h + last_h), 64), side.right(at_h + last_h)),
    )
    put(
        2 * W + 1,
        jnp.where(first, side.left(at_d), roll(side.right_divergence(at_d), 64)),
        jnp.where(first, roll(side.left(at_d + last_h), 64), side.right_divergence(at_d + last_h)),
    )
    put(2 * W + 2, cx_ref[0:8, :], cx_ref[rows - 8 : rows, :])
    put(2 * W + 3, cy_ref[0:8, :], cy_ref[rows - 8 : rows, :])

    def gathered(pieces):
        result = pieces[0]
        for k, piece in enumerate(pieces[1:], 1):
            result = jnp.where(group == k, roll(piece, W * k), result)
        return result

    g_left, g_right = side.left(at_g), side.right(at_g)
    put(
        2 * W + 4,
        gathered([side.left(at_cx), side.right(at_cx), side.left(at_cy), side.right(at_cy), g_left, g_right]),
        gathered(
            [roll(side.left(at_cx + last_c), W), roll(side.right(at_cx + last_c), W)]
            + [roll(side.left(at_cy + last_c), W), roll(side.right(at_cy + last_c), W)]
            + [g_left, g_right]
        ),
    )
    put(2 * W + 5, d_ref[rows], d_ref[rows])
    store.release()


MESSAGE = 2 * W + 6


def strips_kernel(
    rows, even_in, odd_in, even_out, odd_out, h_ref, d_ref, cx_ref, cy_ref, done_ref, wet_ref, uplift_ref,
    merged, bh0, bd0, cbx, cby, sums, hb, db, lefts, rights,
):
    side = Sides(even_in, odd_in, even_out, odd_out)
    lane = side.lane
    second = second_lanes(lane)
    at_h, at_d, at_cx, at_cy, at_g = payload_layout(rows)
    count = rows // 2 + W
    offset = rows // 2 - W
    store = Stores(24)
    for place in range(at_g + 1):
        store(lefts, place, side.left(place))
        right = side.right_divergence(place) if at_d <= place < at_cx else side.right(place)
        store(rights, place, right)
    store.release()

    for ref, target, place in ((cx_ref, cbx, at_cx), (cy_ref, cby, at_cy)):

        def strip_tile(row, shift):
            p, k = divmod(row // 8, GROUPS)
            left = roll(lefts[place + p], 64 - W - W * k + shift)
            right = roll(rights[place + p], shift - W * k)
            return strip(lane, ref[pl.ds(row, 8), :], left, right, shift)

        for row in range(0, count, 8):
            value = jnp.where(second, strip_tile(row + offset, SECOND), strip_tile(row, 0))
            store(target, pl.ds(row, 8), value)

    def strips_at(row, m, k, shift):
        left, right = lefts[at_h + m], rights[at_h + m]
        left, right = roll(left, 64 - W - W * k + shift), roll(right, shift - W * k)
        height = strip(lane, h_ref[row], left, right, shift)
        left, right = lefts[at_d + m], rights[at_d + m]
        left, right = roll(left, 64 - W + 1 - W * k + shift), roll(right, shift - W * k)
        return height, strip_divergence(lane, d_ref[row], left, right, shift)

    def build(b, length):
        for k in range(length):
            row = b * GROUPS + k
            upper = strips_at(row, b, k, 0)
            lower_m, lower_k = divmod(offset + k, GROUPS)
            lower = strips_at(row + offset, b + lower_m, lower_k, SECOND)
            store(bh0, row, jnp.where(second, lower[0], upper[0]))
            store(bd0, row, jnp.where(second, lower[1], upper[1]))

    for b in range(0, count, GROUPS):
        build(b // GROUPS, min(GROUPS, count - b))
    store.release()
    bd0[count] = strip(lane, d_ref[rows], roll(lefts[at_g], 64 - W), rights[at_g])
    first = (bh0, bd0, hb, db, cbx, cby)
    then = (hb, db, hb, db, cbx, cby)
    run_steps(count, range(ITERS), first, then, 24)

    bounds = slot_bounds(rows)
    for u in range(len(bounds) - 1):
        total = jnp.zeros((8, LANES), F32)
        for r in range(max(bounds[u], W), min(bounds[u + 1], rows - W)):
            lower = r >= rows // 2
            value = merge(lane, done_ref[r], hb[r - offset if lower else r], lower)
            store(merged, r, value)
            weight = wet_ref[pl.ds(r, 1), :].astype(F32) * uplift_ref[pl.ds(r, 1), :] * (1.0 / BS)
            total = total + weight * value
        store(sums, u, total)
    store.release()


def slot_bounds(length):
    return [0] + list(range(BS // 2, length, BS)) + [length]


def bands_kernel(
    rows, x_even_in, x_odd_in, h_ref, d_ref, cx_ref, cy_ref, bh0, bd0, cbx, cby, done_wet, uplift_ref, sums_ref, homes_ref,
    edge, message, hs, ds, cxs, cys,
):
    lane = lanes_of()
    second = second_lanes(lane)
    even = lax.rem(lax.axis_index("gx"), 2) == 0
    depth = 3 * W
    count = rows // 2 + W

    def above(place):
        return jnp.where(even, x_odd_in[place], x_even_in[place])

    def below(place):
        return jnp.where(even, x_even_in[place], x_odd_in[place])

    def both(upper, lower):
        return jnp.where(second, lower, upper)

    store = Stores(24)

    top, bottom, strips = 0, 1, 2
    for c, (ref, mine, packed) in enumerate(((cxs, cx_ref, cbx), (cys, cy_ref, cby))):
        halos = []
        for got, shift in ((above, 0), (below, SECOND)):
            value, corner = got(2 * W + 2 + c), got(2 * W + 4)
            left = roll(corner, 64 - W - 2 * W * c + shift)
            right = roll(corner, shift - W - 2 * W * c)
            halos.append((value, strip(lane, value, left, right, shift)))
        store(ref, (top, slice(0, W)), halos[0][0])
        store(ref, (top, slice(W, depth)), mine[0 : 2 * W, :])
        store(ref, (bottom, slice(0, 2 * W)), mine[rows - 2 * W : rows, :])
        store(ref, (bottom, slice(2 * W, depth)), halos[1][0])
        store(ref, (strips, slice(0, W)), both(halos[0][1], packed[count - 2 * W : count - W, :]))
        store(ref, (strips, slice(W, 2 * W)), both(packed[0:W, :], packed[count - W : count, :]))
        store(
            ref, (strips, slice(2 * W, depth)), both(packed[W : 2 * W, :], halos[1][1])
        )

    def halo_strips(got, j, shift):
        packed_h, packed_d = got(2 * W), got(2 * W + 1)
        left, right = roll(packed_h, 64 - W - W * j + shift), roll(packed_h, shift - 64 - W * j)
        height = strip(lane, got(j), left, right, shift)
        left, right = roll(packed_d, 64 - W + 1 - W * j + shift), roll(packed_d, shift - 64 - W * j)
        return height, strip_divergence(lane, got(W + j), left, right, shift)

    flux, corner = above(2 * W + 5), above(2 * W + 4)
    flux_strip = strip(lane, flux, roll(corner, 64 - W - 4 * W), roll(corner, -5 * W))
    for j in range(W):
        upper, (h_last, d_last) = halo_strips(above, j, 0), halo_strips(below, j, SECOND)
        d_first, d_below = bd0[j], below(W + j)
        d_top = d_ref[j]
        if j == 0:
            d_first = d_first + flux_strip
            d_top = d_top + flux
            d_below = d_below + d_ref[rows]
            d_last = d_last + roll(bd0[count], SECOND)
        low, packed_low = rows - 2 * W + j, count - 2 * W + j
        for band, place, height, divergence in (
            (top, j, above(j), above(W + j)),
            (top, W + j, h_ref[j], d_top),
            (top, 2 * W + j, h_ref[W + j], d_ref[W + j]),
            (bottom, j, h_ref[low], d_ref[low]),
            (bottom, W + j, h_ref[low + W], d_ref[low + W]),
            (bottom, 2 * W + j, below(j), d_below),
            (strips, j, both(upper[0], bh0[packed_low]), both(upper[1], bd0[packed_low])),
            (strips, W + j, both(bh0[j], bh0[packed_low + W]), both(d_first, bd0[packed_low + W])),
            (strips, 2 * W + j, both(bh0[W + j], h_last), both(bd0[W + j], d_last)),
        ):
            store(hs, (band, place), height)
            store(ds, (band, place), divergence)
    store.release()

    views = [(hs.at[b], ds.at[b], hs.at[b], ds.at[b], cxs.at[b], cys.at[b]) for b in range(3)]
    items = []
    for t in range(1, ITERS + 1):
        low, high = t, depth - t
        for view in views:
            for r in range(low, high):
                items.append(view + (r, r == low, "item" if r + 1 < high else "row"))
    advance(items, 8)

    bounds = slot_bounds(rows)
    slots_x = len(bounds) - 1
    totals = [sums_ref[u] for u in range(slots_x)]
    for band, first in ((top, 0), (bottom, rows - W)):
        slot = 0 if band == top else slots_x - 1
        for j in range(W):
            value = merge(lane, hs[band, W + j], hs[strips, W + j], band == bottom)
            store(edge, band * W + j, value)
            weight = done_wet[pl.ds(first + j, 1), :].astype(F32) * uplift_ref[pl.ds(first + j, 1), :] * (1.0 / BS)
            totals[slot] = totals[slot] + weight * value
    store.release()
    column_bounds = slot_bounds(LANES)
    slots_y = len(column_bounds) - 1
    devices = message.shape[0]
    gauge = lax.broadcasted_iota(jnp.int32, (8, LANES), 0)
    shape = (devices, LANES)
    here = lanes_of(shape)
    per_device = 8
    home_of = jnp.where(
        here < per_device * 8,
        lax.broadcasted_iota(jnp.int32, shape, 0) * per_device + here // 8,
        -1,
    )
    built = jnp.zeros(shape, F32)
    for u in range(slots_x):
        for w in range(slots_y):
            inside = (lane >= column_bounds[w]) & (lane < column_bounds[w + 1])
            total = jnp.sum(jnp.where(inside, totals[u], 0.0), axis=1, keepdims=True)
            spread = jnp.sum(jnp.where(lane % 8 == gauge, total, 0.0), axis=0, keepdims=True)
            home = homes_ref[pl.ds(u * slots_y + w, 1), :]
            built = built + jnp.where(home_of == home, spread, 0.0)
    message[...] = built


def write_kernel(rows, merged, edge, out_hbm, sems):
    inner = rows - 2 * W
    copies = []
    for g in range(8):
        for source, at, first, length in (
            (merged, W, W, inner),
            (edge, 0, 0, W),
            (edge, W, rows - W, W),
        ):
            copies.append(
                pltpu.make_async_copy(
                    source.at[pl.ds(at, length), g],
                    out_hbm.at[pl.ds(g * rows + first, length)],
                    sems.at[len(copies)],
                )
            )
    for copy in copies:
        copy.start()
    for copy in copies:
        copy.wait()


def pairs(axis, first):
    return [
        pair
        for i in range(first, lax.axis_size(axis) - 1, 2)
        for pair in ((i, i + 1), (i + 1, i))
    ]


def in_vmem(*arrays):
    return [pltpu.with_memory_space_constraint(array, pltpu.VMEM) for array in arrays]


def in_hbm(array):
    return pltpu.with_memory_space_constraint(array, pltpu.HBM)


def shaped(*shape, dtype=F32):
    return jax.ShapeDtypeStruct(shape, dtype)


def bind(kernel, *sizes):
    def bound(*refs):
        kernel(*sizes, *refs)

    return bound


def body(
    terminal_elevation,
    terminal_flux_x,
    terminal_flux_y,
    courant_x,
    courant_y,
    land_sea,
    uplift,
    tile_patches,
    patch_home,
):
    gauges, rows, columns = terminal_elevation.shape
    flat = (gauges * rows, columns)
    layers = (rows + 8, gauges, columns)
    devices = lax.axis_size("gx") * lax.axis_size("gy")
    slots = tile_patches.shape[2]
    slots_x = len(slot_bounds(rows)) - 1
    vectors = payload_layout(rows)[-1] + 1
    field = pltpu.VMEM((rows, gauges, columns), F32)
    work = pltpu.VMEM(layers, F32)

    height, divergence, odd_out, even_out, courant_x, courant_y, homes = pl.pallas_call(
        bind(load_kernel, rows),
        out_shape=(
            shaped(*layers), shaped(*layers), shaped(vectors, 8, columns), shaped(vectors, 8, columns),
            shaped(rows, columns), shaped(rows, columns), shaped(slots, columns, dtype=jnp.int32),
        ),
        in_specs=[HBM] * 8,
        out_specs=(VMEM,) * 7,
        scratch_shapes=[field] * 3
        + [
            pltpu.VMEM((rows, columns), jnp.int32),
            pltpu.SMEM(tile_patches.shape, jnp.int32),
            pltpu.SMEM(patch_home.shape, jnp.int32),
            pltpu.SemaphoreType.DMA((9,)),
        ],
        compiler_params=params(LOAD_MIB),
        name="load",
    )(
        in_hbm(terminal_elevation.reshape(flat)),
        in_hbm(terminal_flux_x.reshape(flat)),
        in_hbm(terminal_flux_y.reshape(flat)),
        in_hbm(courant_x),
        in_hbm(courant_y),
        in_hbm(land_sea),
        in_hbm(tile_patches),
        in_hbm(patch_home),
    )
    odd_in = lax.ppermute(odd_out, "gy", pairs("gy", 1))
    even_in = lax.ppermute(even_out, "gy", pairs("gy", 0))

    center_h, center_d, token = pl.pallas_call(
        bind(center_first_kernel, rows, range(EARLY)),
        out_shape=(shaped(*layers), shaped(*layers), shaped(8, columns)),
        in_specs=[VMEM] * 4,
        out_specs=(VMEM,) * 3,
        compiler_params=params(2),
        cost_estimate=pl.CostEstimate(flops=COST, bytes_accessed=2**20, transcendentals=0),
        name="center_first",
    )(*in_vmem(height, divergence, courant_x, courant_y))

    x_even_out, x_odd_out = pl.pallas_call(
        bind(middle_kernel, rows),
        out_shape=(shaped(MESSAGE, 8, columns),) * 2,
        in_specs=[VMEM] * 9,
        out_specs=(VMEM,) * 2,
        compiler_params=params(2),
        name="middle",
    )(*in_vmem(even_in, odd_in, even_out, odd_out, height, divergence, courant_x, courant_y, token))
    x_even_in = lax.ppermute(x_even_out, "gx", pairs("gx", 0))
    x_odd_in = lax.ppermute(x_odd_out, "gx", pairs("gx", 1))

    center, _ = pl.pallas_call(
        bind(center_second_kernel, rows, range(EARLY, ITERS)),
        out_shape=(shaped(*layers),) * 2,
        in_specs=[VMEM] * 4,
        out_specs=(VMEM,) * 2,
        input_output_aliases={0: 0, 1: 1},
        compiler_params=params(2),
        cost_estimate=pl.CostEstimate(flops=COST, bytes_accessed=2**20, transcendentals=0),
        name="center_second",
    )(*in_vmem(center_h, center_d, courant_x, courant_y))

    count = rows // 2 + W
    packed = (count + 8, gauges, columns)
    merged, bh0, bd0, cbx, cby, sums = pl.pallas_call(
        bind(strips_kernel, rows),
        out_shape=(
            shaped(rows, gauges, columns), shaped(*packed), shaped(*packed), shaped(count, columns), shaped(count, columns),
            shaped(slots_x, 8, columns),
        ),
        in_specs=[VMEM] * 11,
        out_specs=(VMEM,) * 6,
        scratch_shapes=[pltpu.VMEM(packed, F32)] * 2 + [pltpu.VMEM((vectors, 8, columns), F32)] * 2,
        compiler_params=params(5),
        cost_estimate=pl.CostEstimate(flops=COST, bytes_accessed=2**20, transcendentals=0),
        name="strips",
    )(
        *in_vmem(even_in, odd_in, even_out, odd_out, height, divergence, courant_x, courant_y, center),
        land_sea, uplift,
    )

    depth = 3 * W
    edge, message = pl.pallas_call(
        bind(bands_kernel, rows),
        out_shape=(shaped(2 * W, gauges, columns), shaped(devices, columns)),
        in_specs=[VMEM] * 14,
        out_specs=(VMEM,) * 2,
        scratch_shapes=[
            pltpu.VMEM((3, depth, 8, columns), F32),
            pltpu.VMEM((3, depth, 8, columns), F32),
            pltpu.VMEM((3, depth, columns), F32),
            pltpu.VMEM((3, depth, columns), F32),
        ],
        compiler_params=params(2),
        name="bands",
    )(
        *in_vmem(x_even_in, x_odd_in, height, divergence, courant_x, courant_y, bh0, bd0, cbx, cby),
        land_sea, uplift, *in_vmem(sums, homes),
    )
    received = lax.all_to_all(message, ("gx", "gy"), 0, 0, tiled=True)
    out = pl.pallas_call(
        bind(write_kernel, rows),
        out_shape=shaped(*flat),
        in_specs=[VMEM] * 2,
        out_specs=HBM,
        scratch_shapes=[pltpu.SemaphoreType.DMA((24,))],
        compiler_params=params(1),
        name="write",
    )(*in_vmem(merged, edge))
    per_device = patch_home.shape[0] // devices
    gradient = jnp.sum(received, axis=0)[: per_device * gauges].reshape(per_device, gauges)
    return (out.reshape(gauges, rows, columns), gradient)


LOAD_MIB = 6
COST = 40_000_000
EARLY = 5


def solution(mesh):
    in_specs = (
        P(None, "gx", "gy"),
        P(None, "gx", "gy"),
        P(None, "gx", "gy"),
        P("gx", "gy"),
        P("gx", "gy"),
        P("gx", "gy"),
        P("gx", "gy"),
        P(),
        P(),
    )
    out_specs = (P(None, "gx", "gy"), P(("gx", "gy"), None))
    return jax.shard_map(body, mesh=mesh, in_specs=in_specs, out_specs=out_specs, check_vma=False)
```

```python
import jax
import jax.numpy as jnp
from jax import lax
from jax.experimental import pallas as pl
from jax.experimental.pallas import tpu as pltpu
from jax.sharding import PartitionSpec as P

BS = 64
ITERS = 8
LANES = 128
W = 8
GROUPS = LANES // W
F32 = jnp.float32
VMEM = pl.BlockSpec(memory_space=pltpu.VMEM)
HBM = pl.BlockSpec(memory_space=pl.ANY)


def lanes_of(shape=(8, LANES)):
    return lax.broadcasted_iota(jnp.int32, shape, len(shape) - 1)


def roll(vector, distance):
    distance = distance % LANES
    return pltpu.roll(vector, distance, vector.ndim - 1) if distance else vector


def params(mebibytes):
    return pltpu.CompilerParams(vmem_limit_bytes=mebibytes * 2**20)


def tile(ref, row):
    return ref[pl.ds(row if isinstance(row, int) else pl.multiple_of(row, 8), 8), :]


def payload_layout(rows):
    heights = rows // GROUPS
    tiles = rows // 8 // GROUPS
    return (0, heights, 2 * heights, 2 * heights + tiles, 2 * heights + 2 * tiles)


def advance(items, lag):
    live = {}
    written = {}
    for i in range(-2 * lag, len(items)):
        if i + 2 * lag < len(items):
            h_in, _, _, _, _, _, r, has_above, below, *beside = items[i + 2 * lag]
            assert written.get((id(h_in), r), -(10**9)) < i
            height = h_in[r]
            live[i + 2 * lag] = [
                height,
                roll(height, LANES - 1),
                h_in[r - 1] if has_above else None,
                h_in[r + 1] if below == "row" else None,
                None,
                roll(height, 1) if beside else None,
            ]
        if 0 <= i + lag < len(items):
            state = live[i + lag]
            coef_y, r = items[i + lag][5], items[i + lag][6]
            along = coef_y[pl.ds(r, 1), :] * (state[1] - state[0])
            state[4] = along
            if len(items[i + lag]) > 9:
                state[5] = items[i + lag][9][pl.ds(r, 1), :] * (state[0] - state[5])
            else:
                state[5] = roll(along, 1)
        if i >= 0:
            h_in, d_in, h_out, d_out, coef_x, _, r, has_above, below = items[i][:9]
            height, _, above, under, along, along_before = live.pop(i)
            if below == "item":
                under = live[i + 1][0]
            if has_above:
                before = coef_x[pl.ds(r - 1, 1), :] * (height - above)
            elif i == 0 or items[i - 1][8] != "item":
                before = None
            flux = coef_x[pl.ds(r, 1), :] * ((under - height) if under is not None else -height)
            change = along - along_before + (flux if before is None else flux - before)
            divergence = d_in[r] + change
            d_out[r] = divergence
            h_out[r] = height + divergence
            written[(id(h_out), r)] = i
            before = flux


class Stores:
    def __init__(self, lag):
        self.lag, self.waiting = lag, []

    def __call__(self, ref, place, value):
        self.waiting.append((ref, place, value))
        if len(self.waiting) > self.lag:
            self.release(1)

    def release(self, count=None):
        for ref, place, value in self.waiting[:count]:
            ref[place] = value
        self.waiting = self.waiting[count:] if count else []


def run_steps(count, steps, first, then, lag):
    items = []
    for t in steps:
        refs = first if t == steps[0] else then
        for r in range(t, count - t):
            items.append(refs + (r, t > 0, "item" if r + 1 < count - t else "row" if t else None))
    advance(items, lag)


def load_kernel(
    rows, h_hbm, x_hbm, y_hbm, cx_hbm, cy_hbm, wet_hbm, lists_hbm, home_hbm,
    h_out, d_out, odd_out, even_out, cx_ref, cy_ref, homes, hb, xb, yb, wet_ref, lists_ref, home_ref, sems,
):
    gauges = 8
    parts = 4
    size = rows // parts
    plain = [
        pltpu.make_async_copy(source, target, sems.at[parts + i])
        for i, (source, target) in enumerate(((cx_hbm, cx_ref), (cy_hbm, cy_ref), (wet_hbm, wet_ref)))
    ]
    scalars = [
        pltpu.make_async_copy(lists_hbm, lists_ref, sems.at[parts + 3]),
        pltpu.make_async_copy(home_hbm, home_ref, sems.at[parts + 4]),
    ]
    for copy in plain + scalars:
        copy.start()
    for part in range(parts):
        for source, target in ((y_hbm, yb), (x_hbm, xb), (h_hbm, hb)):
            for gauge in range(gauges):
                pltpu.make_async_copy(
                    source.at[pl.ds(gauge * rows + part * size, size)],
                    target.at[pl.ds(part * size, size), gauge],
                    sems.at[part],
                ).start()

    even = lax.rem(lax.axis_index("gy"), 2) == 0
    lane = lanes_of()
    group = lane // W
    at_h, at_d, at_cx, at_cy, at_g = payload_layout(rows)

    def put(place, to_left, to_right):
        even_out[place] = jnp.where(even, to_right, to_left)
        odd_out[place] = jnp.where(even, to_left, to_right)

    for copy in plain:
        copy.wait()
    for ref, place in ((cx_ref, at_cx), (cy_ref, at_cy)):
        for p in range(rows // 8 // GROUPS):
            to_left = to_right = jnp.zeros((8, LANES), F32)
            for k in range(GROUPS):
                value = ref[pl.ds((p * GROUPS + k) * 8, 8), :]
                to_left = jnp.where(group == k, roll(value, W * k), to_left)
                to_right = jnp.where(group == k, roll(value, W * k + W), to_right)
            put(place + p, to_left, to_right)

    state = {}

    def early(r):
        along_y = cy_ref[pl.ds(r, 1), :] * yb[r]
        state[r] = (along_y, roll(along_y, 1))

    def late(r, above, sides):
        along_y, before_y = state.pop(r)
        along_x = cx_ref[pl.ds(r, 1), :] * xb[r]
        height = wet_ref[pl.ds(r, 1), :].astype(F32) * hb[r]
        part = along_y + along_x if above is None else along_y + (along_x - above)
        divergence = part - jnp.where(lane == 0, 0.0, before_y)
        outgoing = jnp.where(lane == 0, -before_y, divergence)
        h_out[r] = height
        d_out[r] = divergence
        k = r % GROUPS
        mine = group == k
        new = (
            roll(height, W * k),
            roll(divergence, W * k),
            roll(height, W * k + W),
            roll(outgoing, W * k + W - 1),
        )
        sides = new if k == 0 else tuple(jnp.where(mine, n, s) for n, s in zip(new, sides))
        if k == GROUPS - 1:
            put(at_h + r // GROUPS, sides[0], sides[2])
            put(at_d + r // GROUPS, sides[1], sides[3])
        return along_x, sides

    above, sides = None, None
    lag = 16
    for part in range(parts):
        done = hb.at[pl.ds(0, 3 * size)]
        pltpu.make_async_copy(done, done, sems.at[part]).wait()
        low, high = part * size, (part + 1) * size
        for r in range(low - lag, high):
            if r + lag < high:
                early(r + lag)
            if r >= low:
                above, sides = late(r, above, sides)
    d_out[rows] = -above
    put(at_g, -above, roll(-above, W))

    for copy in scalars:
        copy.wait()
    tile_row, tile_column = lax.axis_index("gx"), lax.axis_index("gy")
    for slot in range(homes.shape[0]):
        patch = lists_ref[tile_row, tile_column, slot]
        homes[pl.ds(slot, 1), :] = jnp.full((1, LANES), home_ref[patch], jnp.int32)


def center_first_kernel(rows, steps, h_ref, d_ref, cx_ref, cy_ref, h_out, d_out, token):
    first = (h_ref, d_ref, h_out, d_out, cx_ref, cy_ref)
    then = (h_out, d_out, h_out, d_out, cx_ref, cy_ref)
    run_steps(rows, steps, first, then, 32)
    token[...] = jnp.zeros((8, LANES), F32)


def center_second_kernel(rows, steps, h_in, d_in, cx_ref, cy_ref, h_out, d_out):
    then = (h_out, d_out, h_out, d_out, cx_ref, cy_ref)
    run_steps(rows, steps, then, then, 32)


SECOND = 32


def strip(lane, own, from_left, from_right, shift=0):
    at = (lane - shift) % LANES
    return jnp.where(
        at >= LANES - 2 * W,
        roll(own, shift),
        jnp.where(at < W, from_right, jnp.where(at < 64, from_left, roll(own, 64 + shift))),
    )


def strip_divergence(lane, own, from_left, from_right, shift=0):
    at = (lane - shift) % LANES
    middle = jnp.where(at >= 64, roll(own, 64 + shift), 0.0) + jnp.where(
        (at > 64 - W) & (at <= 64), from_left, 0.0
    )
    return jnp.where(at >= LANES - 2 * W, roll(own, shift), jnp.where(at < W, from_right, middle))


def second_lanes(lane):
    return ((lane >= 16) & (lane < 40)) | ((lane >= 88) & (lane < 112))


def merge(lane, center, packed, lower):
    shift = SECOND if lower else 0
    left, right = roll(packed, 64 - shift), roll(packed, -shift)
    return jnp.where(lane < W, left, jnp.where(lane >= LANES - W, right, center))


class Sides:
    def __init__(self, even_in, odd_in, even_out, odd_out):
        self.even = lax.rem(lax.axis_index("gy"), 2) == 0
        self.lane = lanes_of()
        self.refs = (even_in, odd_in, even_out, odd_out)

    def left(self, place):
        even_in, odd_in, _, _ = self.refs
        return jnp.where(self.even, odd_in[place], even_in[place])

    def right(self, place):
        even_in, odd_in, _, _ = self.refs
        return jnp.where(self.even, even_in[place], odd_in[place])

    def right_divergence(self, place):
        _, _, even_out, odd_out = self.refs
        sent = jnp.where(self.even, even_out[place], odd_out[place])
        return self.right(place) + jnp.where(self.lane % W == 0, roll(sent, -(W - 1)), 0.0)


def middle_kernel(rows, even_in, odd_in, even_out, odd_out, h_ref, d_ref, cx_ref, cy_ref, token, x_even, x_odd):
    side = Sides(even_in, odd_in, even_out, odd_out)
    lane, group = side.lane, side.lane // W
    at_h, at_d, at_cx, at_cy, at_g = payload_layout(rows)
    last_h, last_c = rows // GROUPS - 1, rows // 8 // GROUPS - 1
    even = lax.rem(lax.axis_index("gx"), 2) == 0
    store = Stores(24)

    def put(place, up, down):
        store(x_even, place, jnp.where(even, down, up))
        store(x_odd, place, jnp.where(even, up, down))

    for j in range(W):
        put(j, h_ref[j], h_ref[rows - W + j])
        put(W + j, d_ref[j], d_ref[rows - W + j])
    first = lane < 64
    put(
        2 * W,
        jnp.where(first, side.left(at_h), roll(side.right(at_h), 64)),
        jnp.where(first, roll(side.left(at_h + last_h), 64), side.right(at_h + last_h)),
    )
    put(
        2 * W + 1,
        jnp.where(first, side.left(at_d), roll(side.right_divergence(at_d), 64)),
        jnp.where(first, roll(side.left(at_d + last_h), 64), side.right_divergence(at_d + last_h)),
    )
    put(2 * W + 2, cx_ref[0:8, :], cx_ref[rows - 8 : rows, :])
    put(2 * W + 3, cy_ref[0:8, :], cy_ref[rows - 8 : rows, :])

    def gathered(pieces):
        result = pieces[0]
        for k, piece in enumerate(pieces[1:], 1):
            result = jnp.where(group == k, roll(piece, W * k), result)
        return result

    g_left, g_right = side.left(at_g), side.right(at_g)
    put(
        2 * W + 4,
        gathered([side.left(at_cx), side.right(at_cx), side.left(at_cy), side.right(at_cy), g_left, g_right]),
        gathered(
            [roll(side.left(at_cx + last_c), W), roll(side.right(at_cx + last_c), W)]
            + [roll(side.left(at_cy + last_c), W), roll(side.right(at_cy + last_c), W)]
            + [g_left, g_right]
        ),
    )
    put(2 * W + 5, d_ref[rows], d_ref[rows])
    store.release()


MESSAGE = 2 * W + 6


def strips_kernel(
    rows, even_in, odd_in, even_out, odd_out, h_ref, d_ref, cx_ref, cy_ref, done_ref, wet_ref, uplift_ref,
    merged, bh0, bd0, cbx, cby, sums, hb, db, lefts, rights,
):
    side = Sides(even_in, odd_in, even_out, odd_out)
    lane = side.lane
    second = second_lanes(lane)
    at_h, at_d, at_cx, at_cy, at_g = payload_layout(rows)
    count = rows // 2 + W
    offset = rows // 2 - W
    store = Stores(24)
    for place in range(at_g + 1):
        store(lefts, place, side.left(place))
        right = side.right_divergence(place) if at_d <= place < at_cx else side.right(place)
        store(rights, place, right)
    store.release()

    for ref, target, place in ((cx_ref, cbx, at_cx), (cy_ref, cby, at_cy)):

        def strip_tile(row, shift):
            p, k = divmod(row // 8, GROUPS)
            left = roll(lefts[place + p], 64 - W - W * k + shift)
            right = roll(rights[place + p], shift - W * k)
            return strip(lane, ref[pl.ds(row, 8), :], left, right, shift)

        for row in range(0, count, 8):
            value = jnp.where(second, strip_tile(row + offset, SECOND), strip_tile(row, 0))
            store(target, pl.ds(row, 8), value)

    def strips_at(row, m, k, shift):
        left, right = lefts[at_h + m], rights[at_h + m]
        left, right = roll(left, 64 - W - W * k + shift), roll(right, shift - W * k)
        height = strip(lane, h_ref[row], left, right, shift)
        left, right = lefts[at_d + m], rights[at_d + m]
        left, right = roll(left, 64 - W + 1 - W * k + shift), roll(right, shift - W * k)
        return height, strip_divergence(lane, d_ref[row], left, right, shift)

    def build(b, length):
        for k in range(length):
            row = b * GROUPS + k
            upper = strips_at(row, b, k, 0)
            lower_m, lower_k = divmod(offset + k, GROUPS)
            lower = strips_at(row + offset, b + lower_m, lower_k, SECOND)
            store(bh0, row, jnp.where(second, lower[0], upper[0]))
            store(bd0, row, jnp.where(second, lower[1], upper[1]))

    for b in range(0, count, GROUPS):
        build(b // GROUPS, min(GROUPS, count - b))
    store.release()
    bd0[count] = strip(lane, d_ref[rows], roll(lefts[at_g], 64 - W), rights[at_g])
    first = (bh0, bd0, hb, db, cbx, cby)
    then = (hb, db, hb, db, cbx, cby)
    run_steps(count, range(ITERS), first, then, 24)

    bounds = slot_bounds(rows)
    for u in range(len(bounds) - 1):
        total = jnp.zeros((8, LANES), F32)
        for r in range(max(bounds[u], W), min(bounds[u + 1], rows - W)):
            lower = r >= rows // 2
            value = merge(lane, done_ref[r], hb[r - offset if lower else r], lower)
            store(merged, r, value)
            weight = wet_ref[pl.ds(r, 1), :].astype(F32) * uplift_ref[pl.ds(r, 1), :] * (1.0 / BS)
            total = total + weight * value
        store(sums, u, total)
    store.release()


def slot_bounds(length):
    return [0] + list(range(BS // 2, length, BS)) + [length]


def bands_kernel(
    rows, x_even_in, x_odd_in, h_ref, d_ref, cx_ref, cy_ref, bh0, bd0, cbx, cby, done_wet, uplift_ref, sums_ref, homes_ref,
    edge, message, hs, ds, cxs, cys, cbs,
):
    lane = lanes_of()
    second = second_lanes(lane)
    even = lax.rem(lax.axis_index("gx"), 2) == 0
    depth = 3 * W
    count = rows // 2 + W

    def above(place):
        return jnp.where(even, x_odd_in[place], x_even_in[place])

    def below(place):
        return jnp.where(even, x_even_in[place], x_odd_in[place])

    def both(upper, lower):
        return jnp.where(second, lower, upper)

    store = Stores(24)

    top, bottom, strips = 0, 1, 2
    for c, (ref, mine, packed) in enumerate(((cxs, cx_ref, cbx), (cys, cy_ref, cby))):
        halos = []
        for got, shift in ((above, 0), (below, SECOND)):
            value, corner = got(2 * W + 2 + c), got(2 * W + 4)
            left = roll(corner, 64 - W - 2 * W * c + shift)
            right = roll(corner, shift - W - 2 * W * c)
            halos.append((value, strip(lane, value, left, right, shift)))
        store(ref, (top, slice(0, W)), halos[0][0])
        store(ref, (top, slice(W, depth)), mine[0 : 2 * W, :])
        store(ref, (bottom, slice(0, 2 * W)), mine[rows - 2 * W : rows, :])
        store(ref, (bottom, slice(2 * W, depth)), halos[1][0])
        store(ref, (strips, slice(0, W)), both(halos[0][1], packed[count - 2 * W : count - W, :]))
        store(ref, (strips, slice(W, 2 * W)), both(packed[0:W, :], packed[count - W : count, :]))
        store(
            ref, (strips, slice(2 * W, depth)), both(packed[W : 2 * W, :], halos[1][1])
        )

    def halo_strips(got, j, shift):
        packed_h, packed_d = got(2 * W), got(2 * W + 1)
        left, right = roll(packed_h, 64 - W - W * j + shift), roll(packed_h, shift - 64 - W * j)
        height = strip(lane, got(j), left, right, shift)
        left, right = roll(packed_d, 64 - W + 1 - W * j + shift), roll(packed_d, shift - 64 - W * j)
        return height, strip_divergence(lane, got(W + j), left, right, shift)

    flux, corner = above(2 * W + 5), above(2 * W + 4)
    flux_strip = strip(lane, flux, roll(corner, 64 - W - 4 * W), roll(corner, -5 * W))
    for j in range(W):
        upper, (h_last, d_last) = halo_strips(above, j, 0), halo_strips(below, j, SECOND)
        d_first, d_below = bd0[j], below(W + j)
        d_top = d_ref[j]
        if j == 0:
            d_first = d_first + flux_strip
            d_top = d_top + flux
            d_below = d_below + d_ref[rows]
            d_last = d_last + roll(bd0[count], SECOND)
        low, packed_low = rows - 2 * W + j, count - 2 * W + j
        for band, place, height, divergence in (
            (top, j, above(j), above(W + j)),
            (top, W + j, h_ref[j], d_top),
            (top, 2 * W + j, h_ref[W + j], d_ref[W + j]),
            (bottom, j, h_ref[low], d_ref[low]),
            (bottom, W + j, h_ref[low + W], d_ref[low + W]),
            (bottom, 2 * W + j, below(j), d_below),
            (strips, j, both(upper[0], bh0[packed_low]), both(upper[1], bd0[packed_low])),
            (strips, W + j, both(bh0[j], bh0[packed_low + W]), both(d_first, bd0[packed_low + W])),
            (strips, 2 * W + j, both(bh0[W + j], h_last), both(bd0[W + j], d_last)),
        ):
            store(hs, (band, place), height)
            store(ds, (band, place), divergence)
    store.release()

    for b in range(3):
        for low in range(0, depth, W):
            store(cbs, (b, slice(low, low + W)), roll(cys[b, low : low + W, :], 1))
    store.release()
    views = [(hs.at[b], ds.at[b], hs.at[b], ds.at[b], cxs.at[b], cys.at[b]) for b in range(3)]
    items = []
    for t in range(1, ITERS + 1):
        low, high = t, depth - t
        for b, view in enumerate(views):
            for r in range(low, high):
                items.append(view + (r, r == low, "item" if r + 1 < high else "row", cbs.at[b]))
    advance(items, 8)

    bounds = slot_bounds(rows)
    slots_x = len(bounds) - 1
    totals = [sums_ref[u] for u in range(slots_x)]
    for band, first in ((top, 0), (bottom, rows - W)):
        slot = 0 if band == top else slots_x - 1
        for j in range(W):
            value = merge(lane, hs[band, W + j], hs[strips, W + j], band == bottom)
            store(edge, band * W + j, value)
            weight = done_wet[pl.ds(first + j, 1), :].astype(F32) * uplift_ref[pl.ds(first + j, 1), :] * (1.0 / BS)
            totals[slot] = totals[slot] + weight * value
    store.release()
    column_bounds = slot_bounds(LANES)
    slots_y = len(column_bounds) - 1
    devices = message.shape[0]
    gauge = lax.broadcasted_iota(jnp.int32, (8, LANES), 0)
    shape = (devices, LANES)
    here = lanes_of(shape)
    per_device = 8
    home_of = jnp.where(
        here < per_device * 8,
        lax.broadcasted_iota(jnp.int32, shape, 0) * per_device + here // 8,
        -1,
    )
    built = jnp.zeros(shape, F32)
    for u in range(slots_x):
        for w in range(slots_y):
            inside = (lane >= column_bounds[w]) & (lane < column_bounds[w + 1])
            total = jnp.sum(jnp.where(inside, totals[u], 0.0), axis=1, keepdims=True)
            spread = jnp.sum(jnp.where(lane % 8 == gauge, total, 0.0), axis=0, keepdims=True)
            home = homes_ref[pl.ds(u * slots_y + w, 1), :]
            built = built + jnp.where(home_of == home, spread, 0.0)
    message[...] = built


def write_kernel(rows, merged, edge, out_hbm, sems):
    inner = rows - 2 * W
    copies = []
    for g in range(8):
        for source, at, first, length in (
            (merged, W, W, inner),
            (edge, 0, 0, W),
            (edge, W, rows - W, W),
        ):
            copies.append(
                pltpu.make_async_copy(
                    source.at[pl.ds(at, length), g],
                    out_hbm.at[pl.ds(g * rows + first, length)],
                    sems.at[len(copies)],
                )
            )
    for copy in copies:
        copy.start()
    for copy in copies:
        copy.wait()


def pairs(axis, first):
    return [
        pair
        for i in range(first, lax.axis_size(axis) - 1, 2)
        for pair in ((i, i + 1), (i + 1, i))
    ]


def in_vmem(*arrays):
    return [pltpu.with_memory_space_constraint(array, pltpu.VMEM) for array in arrays]


def in_hbm(array):
    return pltpu.with_memory_space_constraint(array, pltpu.HBM)


def shaped(*shape, dtype=F32):
    return jax.ShapeDtypeStruct(shape, dtype)


def bind(kernel, *sizes):
    def bound(*refs):
        kernel(*sizes, *refs)

    return bound


def body(
    terminal_elevation,
    terminal_flux_x,
    terminal_flux_y,
    courant_x,
    courant_y,
    land_sea,
    uplift,
    tile_patches,
    patch_home,
):
    gauges, rows, columns = terminal_elevation.shape
    flat = (gauges * rows, columns)
    layers = (rows + 8, gauges, columns)
    devices = lax.axis_size("gx") * lax.axis_size("gy")
    slots = tile_patches.shape[2]
    slots_x = len(slot_bounds(rows)) - 1
    vectors = payload_layout(rows)[-1] + 1
    field = pltpu.VMEM((rows, gauges, columns), F32)
    work = pltpu.VMEM(layers, F32)

    height, divergence, odd_out, even_out, courant_x, courant_y, homes = pl.pallas_call(
        bind(load_kernel, rows),
        out_shape=(
            shaped(*layers), shaped(*layers), shaped(vectors, 8, columns), shaped(vectors, 8, columns),
            shaped(rows, columns), shaped(rows, columns), shaped(slots, columns, dtype=jnp.int32),
        ),
        in_specs=[HBM] * 8,
        out_specs=(VMEM,) * 7,
        scratch_shapes=[field] * 3
        + [
            pltpu.VMEM((rows, columns), jnp.int32),
            pltpu.SMEM(tile_patches.shape, jnp.int32),
            pltpu.SMEM(patch_home.shape, jnp.int32),
            pltpu.SemaphoreType.DMA((9,)),
        ],
        compiler_params=params(LOAD_MIB),
        name="load",
    )(
        in_hbm(terminal_elevation.reshape(flat)),
        in_hbm(terminal_flux_x.reshape(flat)),
        in_hbm(terminal_flux_y.reshape(flat)),
        in_hbm(courant_x),
        in_hbm(courant_y),
        in_hbm(land_sea),
        in_hbm(tile_patches),
        in_hbm(patch_home),
    )
    odd_in = lax.ppermute(odd_out, "gy", pairs("gy", 1))
    even_in = lax.ppermute(even_out, "gy", pairs("gy", 0))

    center_h, center_d, token = pl.pallas_call(
        bind(center_first_kernel, rows, range(EARLY)),
        out_shape=(shaped(*layers), shaped(*layers), shaped(8, columns)),
        in_specs=[VMEM] * 4,
        out_specs=(VMEM,) * 3,
        compiler_params=params(2),
        cost_estimate=pl.CostEstimate(flops=COST, bytes_accessed=2**20, transcendentals=0),
        name="center_first",
    )(*in_vmem(height, divergence, courant_x, courant_y))

    x_even_out, x_odd_out = pl.pallas_call(
        bind(middle_kernel, rows),
        out_shape=(shaped(MESSAGE, 8, columns),) * 2,
        in_specs=[VMEM] * 9,
        out_specs=(VMEM,) * 2,
        compiler_params=params(2),
        name="middle",
    )(*in_vmem(even_in, odd_in, even_out, odd_out, height, divergence, courant_x, courant_y, token))
    x_even_in = lax.ppermute(x_even_out, "gx", pairs("gx", 0))
    x_odd_in = lax.ppermute(x_odd_out, "gx", pairs("gx", 1))

    center, _ = pl.pallas_call(
        bind(center_second_kernel, rows, range(EARLY, ITERS)),
        out_shape=(shaped(*layers),) * 2,
        in_specs=[VMEM] * 4,
        out_specs=(VMEM,) * 2,
        input_output_aliases={0: 0, 1: 1},
        compiler_params=params(2),
        cost_estimate=pl.CostEstimate(flops=COST, bytes_accessed=2**20, transcendentals=0),
        name="center_second",
    )(*in_vmem(center_h, center_d, courant_x, courant_y))

    count = rows // 2 + W
    packed = (count + 8, gauges, columns)
    merged, bh0, bd0, cbx, cby, sums = pl.pallas_call(
        bind(strips_kernel, rows),
        out_shape=(
            shaped(rows, gauges, columns), shaped(*packed), shaped(*packed), shaped(count, columns), shaped(count, columns),
            shaped(slots_x, 8, columns),
        ),
        in_specs=[VMEM] * 11,
        out_specs=(VMEM,) * 6,
        scratch_shapes=[pltpu.VMEM(packed, F32)] * 2 + [pltpu.VMEM((vectors, 8, columns), F32)] * 2,
        compiler_params=params(5),
        cost_estimate=pl.CostEstimate(flops=COST, bytes_accessed=2**20, transcendentals=0),
        name="strips",
    )(
        *in_vmem(even_in, odd_in, even_out, odd_out, height, divergence, courant_x, courant_y, center),
        land_sea, uplift,
    )

    depth = 3 * W
    edge, message = pl.pallas_call(
        bind(bands_kernel, rows),
        out_shape=(shaped(2 * W, gauges, columns), shaped(devices, columns)),
        in_specs=[VMEM] * 14,
        out_specs=(VMEM,) * 2,
        scratch_shapes=[
            pltpu.VMEM((3, depth, 8, columns), F32),
            pltpu.VMEM((3, depth, 8, columns), F32),
            pltpu.VMEM((3, depth, columns), F32),
            pltpu.VMEM((3, depth, columns), F32),
            pltpu.VMEM((3, depth, columns), F32),
        ],
        compiler_params=params(2),
        name="bands",
    )(
        *in_vmem(x_even_in, x_odd_in, height, divergence, courant_x, courant_y, bh0, bd0, cbx, cby),
        land_sea, uplift, *in_vmem(sums, homes),
    )
    received = lax.all_to_all(message, ("gx", "gy"), 0, 0, tiled=True)
    out = pl.pallas_call(
        bind(write_kernel, rows),
        out_shape=shaped(*flat),
        in_specs=[VMEM] * 2,
        out_specs=HBM,
        scratch_shapes=[pltpu.SemaphoreType.DMA((24,))],
        compiler_params=params(1),
        name="write",
    )(*in_vmem(merged, edge))
    per_device = patch_home.shape[0] // devices
    gradient = jnp.sum(received, axis=0)[: per_device * gauges].reshape(per_device, gauges)
    return (out.reshape(gauges, rows, columns), gradient)


LOAD_MIB = 6
COST = 40_000_000
EARLY = 6


def solution(mesh):
    in_specs = (
        P(None, "gx", "gy"),
        P(None, "gx", "gy"),
        P(None, "gx", "gy"),
        P("gx", "gy"),
        P("gx", "gy"),
        P("gx", "gy"),
        P("gx", "gy"),
        P(),
        P(),
    )
    out_specs = (P(None, "gx", "gy"), P(("gx", "gy"), None))
    return jax.shard_map(body, mesh=mesh, in_specs=in_specs, out_specs=out_specs, check_vma=False)
```

```python
import jax
import jax.numpy as jnp
from jax import lax
from jax.experimental import pallas as pl
from jax.experimental.pallas import tpu as pltpu
from jax.sharding import PartitionSpec as P

BS = 64
ITERS = 8
LANES = 128
W = 8
GROUPS = LANES // W
F32 = jnp.float32
VMEM = pl.BlockSpec(memory_space=pltpu.VMEM)
HBM = pl.BlockSpec(memory_space=pl.ANY)


def lanes_of(shape=(8, LANES)):
    return lax.broadcasted_iota(jnp.int32, shape, len(shape) - 1)


def roll(vector, distance):
    distance = distance % LANES
    return pltpu.roll(vector, distance, vector.ndim - 1) if distance else vector


def params(mebibytes):
    return pltpu.CompilerParams(vmem_limit_bytes=mebibytes * 2**20)


def tile(ref, row):
    return ref[pl.ds(row if isinstance(row, int) else pl.multiple_of(row, 8), 8), :]


def payload_layout(rows):
    heights = rows // GROUPS
    tiles = rows // 8 // GROUPS
    return (0, heights, 2 * heights, 2 * heights + tiles, 2 * heights + 2 * tiles)


def advance(items, lag):
    live = {}
    written = {}
    for i in range(-2 * lag, len(items)):
        if i + 2 * lag < len(items):
            h_in, _, _, _, _, _, r, has_above, below, *beside = items[i + 2 * lag]
            assert written.get((id(h_in), r), -(10**9)) < i
            height = h_in[r]
            live[i + 2 * lag] = [
                height,
                roll(height, LANES - 1),
                h_in[r - 1] if has_above else None,
                h_in[r + 1] if below == "row" else None,
                None,
                roll(height, 1) if beside else None,
            ]
        if 0 <= i + lag < len(items):
            state = live[i + lag]
            coef_y, r = items[i + lag][5], items[i + lag][6]
            along = coef_y[pl.ds(r, 1), :] * (state[1] - state[0])
            state[4] = along
            if len(items[i + lag]) > 9:
                state[5] = items[i + lag][9][pl.ds(r, 1), :] * (state[0] - state[5])
            else:
                state[5] = roll(along, 1)
        if i >= 0:
            h_in, d_in, h_out, d_out, coef_x, _, r, has_above, below = items[i][:9]
            height, _, above, under, along, along_before = live.pop(i)
            if below == "item":
                under = live[i + 1][0]
            if has_above:
                before = coef_x[pl.ds(r - 1, 1), :] * (height - above)
            elif i == 0 or items[i - 1][8] != "item":
                before = None
            flux = coef_x[pl.ds(r, 1), :] * ((under - height) if under is not None else -height)
            change = along - along_before + (flux if before is None else flux - before)
            divergence = d_in[r] + change
            d_out[r] = divergence
            h_out[r] = height + divergence
            written[(id(h_out), r)] = i
            before = flux


class Stores:
    def __init__(self, lag):
        self.lag, self.waiting = lag, []

    def __call__(self, ref, place, value):
        self.waiting.append((ref, place, value))
        if len(self.waiting) > self.lag:
            self.release(1)

    def release(self, count=None):
        for ref, place, value in self.waiting[:count]:
            ref[place] = value
        self.waiting = self.waiting[count:] if count else []


def run_steps(count, steps, first, then, lag):
    items = []
    for t in steps:
        refs = first if t == steps[0] else then
        for r in range(t, count - t):
            items.append(refs + (r, t > 0, "item" if r + 1 < count - t else "row" if t else None))
    advance(items, lag)


def load_kernel(
    rows, h_hbm, x_hbm, y_hbm, cx_hbm, cy_hbm, wet_hbm, lists_hbm, home_hbm,
    h_out, d_out, odd_out, even_out, cx_ref, cy_ref, homes, hb, xb, yb, wet_ref, lists_ref, home_ref, sems,
):
    gauges = 8
    parts, fields = 2, 3
    size = rows // parts
    plain = [
        pltpu.make_async_copy(source, target, sems.at[parts * fields + i])
        for i, (source, target) in enumerate(((cx_hbm, cx_ref), (cy_hbm, cy_ref), (wet_hbm, wet_ref)))
    ]
    scalars = [
        pltpu.make_async_copy(lists_hbm, lists_ref, sems.at[parts * fields + 3]),
        pltpu.make_async_copy(home_hbm, home_ref, sems.at[parts * fields + 4]),
    ]
    for copy in plain + scalars:
        copy.start()
    for part in range(parts):
        for field, (source, target) in enumerate(((y_hbm, yb), (x_hbm, xb), (h_hbm, hb))):
            for gauge in range(gauges):
                pltpu.make_async_copy(
                    source.at[pl.ds(gauge * rows + part * size, size)],
                    target.at[pl.ds(part * size, size), gauge],
                    sems.at[part * fields + field],
                ).start()

    even = lax.rem(lax.axis_index("gy"), 2) == 0
    lane = lanes_of()
    group = lane // W
    at_h, at_d, at_cx, at_cy, at_g = payload_layout(rows)

    def put(place, to_left, to_right):
        even_out[place] = jnp.where(even, to_right, to_left)
        odd_out[place] = jnp.where(even, to_left, to_right)

    for copy in plain:
        copy.wait()
    for ref, place in ((cx_ref, at_cx), (cy_ref, at_cy)):
        for p in range(rows // 8 // GROUPS):
            to_left = to_right = jnp.zeros((8, LANES), F32)
            for k in range(GROUPS):
                value = ref[pl.ds((p * GROUPS + k) * 8, 8), :]
                to_left = jnp.where(group == k, roll(value, W * k), to_left)
                to_right = jnp.where(group == k, roll(value, W * k + W), to_right)
            put(place + p, to_left, to_right)

    state = {}

    def early(r):
        along_y = cy_ref[pl.ds(r, 1), :] * yb[r]
        state[r] = (along_y, roll(along_y, 1))

    def late(r, above, sides):
        along_y, before_y = state.pop(r)
        along_x = cx_ref[pl.ds(r, 1), :] * xb[r]
        height = wet_ref[pl.ds(r, 1), :].astype(F32) * hb[r]
        part = along_y + along_x if above is None else along_y + (along_x - above)
        divergence = part - jnp.where(lane == 0, 0.0, before_y)
        outgoing = jnp.where(lane == 0, -before_y, divergence)
        h_out[r] = height
        d_out[r] = divergence
        k = r % GROUPS
        mine = group == k
        new = (
            roll(height, W * k),
            roll(divergence, W * k),
            roll(height, W * k + W),
            roll(outgoing, W * k + W - 1),
        )
        sides = new if k == 0 else tuple(jnp.where(mine, n, s) for n, s in zip(new, sides))
        if k == GROUPS - 1:
            put(at_h + r // GROUPS, sides[0], sides[2])
            put(at_d + r // GROUPS, sides[1], sides[3])
        return along_x, sides

    above, sides = None, None
    lag = 16
    for part in range(parts):
        for field, target in enumerate((yb, xb, hb)):
            done = target.at[pl.ds(part * size, size)]
            pltpu.make_async_copy(done, done, sems.at[part * fields + field]).wait()
        low, high = part * size, (part + 1) * size
        for r in range(low - lag, high):
            if r + lag < high:
                early(r + lag)
            if r >= low:
                above, sides = late(r, above, sides)
    d_out[rows] = -above
    put(at_g, -above, roll(-above, W))

    for copy in scalars:
        copy.wait()
    tile_row, tile_column = lax.axis_index("gx"), lax.axis_index("gy")
    for slot in range(homes.shape[0]):
        patch = lists_ref[tile_row, tile_column, slot]
        homes[pl.ds(slot, 1), :] = jnp.full((1, LANES), home_ref[patch], jnp.int32)


def center_first_kernel(rows, steps, h_ref, d_ref, cx_ref, cy_ref, h_out, d_out, token):
    first = (h_ref, d_ref, h_out, d_out, cx_ref, cy_ref)
    then = (h_out, d_out, h_out, d_out, cx_ref, cy_ref)
    run_steps(rows, steps, first, then, 32)
    token[...] = jnp.zeros((8, LANES), F32)


def center_second_kernel(rows, steps, h_in, d_in, cx_ref, cy_ref, h_out, d_out):
    then = (h_out, d_out, h_out, d_out, cx_ref, cy_ref)
    run_steps(rows, steps, then, then, 32)


SECOND = 32


def strip(lane, own, from_left, from_right, shift=0):
    at = (lane - shift) % LANES
    return jnp.where(
        at >= LANES - 2 * W,
        roll(own, shift),
        jnp.where(at < W, from_right, jnp.where(at < 64, from_left, roll(own, 64 + shift))),
    )


def strip_divergence(lane, own, from_left, from_right, shift=0):
    at = (lane - shift) % LANES
    middle = jnp.where(at >= 64, roll(own, 64 + shift), 0.0) + jnp.where(
        (at > 64 - W) & (at <= 64), from_left, 0.0
    )
    return jnp.where(at >= LANES - 2 * W, roll(own, shift), jnp.where(at < W, from_right, middle))


def second_lanes(lane):
    return ((lane >= 16) & (lane < 40)) | ((lane >= 88) & (lane < 112))


def merge(lane, center, packed, lower):
    shift = SECOND if lower else 0
    left, right = roll(packed, 64 - shift), roll(packed, -shift)
    return jnp.where(lane < W, left, jnp.where(lane >= LANES - W, right, center))


class Sides:
    def __init__(self, even_in, odd_in, even_out, odd_out):
        self.even = lax.rem(lax.axis_index("gy"), 2) == 0
        self.lane = lanes_of()
        self.refs = (even_in, odd_in, even_out, odd_out)

    def left(self, place):
        even_in, odd_in, _, _ = self.refs
        return jnp.where(self.even, odd_in[place], even_in[place])

    def right(self, place):
        even_in, odd_in, _, _ = self.refs
        return jnp.where(self.even, even_in[place], odd_in[place])

    def right_divergence(self, place):
        _, _, even_out, odd_out = self.refs
        sent = jnp.where(self.even, even_out[place], odd_out[place])
        return self.right(place) + jnp.where(self.lane % W == 0, roll(sent, -(W - 1)), 0.0)


def middle_kernel(rows, even_in, odd_in, even_out, odd_out, h_ref, d_ref, cx_ref, cy_ref, token, x_even, x_odd):
    side = Sides(even_in, odd_in, even_out, odd_out)
    lane, group = side.lane, side.lane // W
    at_h, at_d, at_cx, at_cy, at_g = payload_layout(rows)
    last_h, last_c = rows // GROUPS - 1, rows // 8 // GROUPS - 1
    even = lax.rem(lax.axis_index("gx"), 2) == 0
    store = Stores(24)

    def put(place, up, down):
        store(x_even, place, jnp.where(even, down, up))
        store(x_odd, place, jnp.where(even, up, down))

    for j in range(W):
        put(j, h_ref[j], h_ref[rows - W + j])
        put(W + j, d_ref[j], d_ref[rows - W + j])
    first = lane < 64
    put(
        2 * W,
        jnp.where(first, side.left(at_h), roll(side.right(at_h), 64)),
        jnp.where(first, roll(side.left(at_h + last_h), 64), side.right(at_h + last_h)),
    )
    put(
        2 * W + 1,
        jnp.where(first, side.left(at_d), roll(side.right_divergence(at_d), 64)),
        jnp.where(first, roll(side.left(at_d + last_h), 64), side.right_divergence(at_d + last_h)),
    )
    put(2 * W + 2, cx_ref[0:8, :], cx_ref[rows - 8 : rows, :])
    put(2 * W + 3, cy_ref[0:8, :], cy_ref[rows - 8 : rows, :])

    def gathered(pieces):
        result = pieces[0]
        for k, piece in enumerate(pieces[1:], 1):
            result = jnp.where(group == k, roll(piece, W * k), result)
        return result

    g_left, g_right = side.left(at_g), side.right(at_g)
    put(
        2 * W + 4,
        gathered([side.left(at_cx), side.right(at_cx), side.left(at_cy), side.right(at_cy), g_left, g_right]),
        gathered(
            [roll(side.left(at_cx + last_c), W), roll(side.right(at_cx + last_c), W)]
            + [roll(side.left(at_cy + last_c), W), roll(side.right(at_cy + last_c), W)]
            + [g_left, g_right]
        ),
    )
    put(2 * W + 5, d_ref[rows], d_ref[rows])
    store.release()


MESSAGE = 2 * W + 6


def strips_kernel(
    rows, even_in, odd_in, even_out, odd_out, h_ref, d_ref, cx_ref, cy_ref, done_ref, wet_ref, uplift_ref,
    merged, bh0, bd0, cbx, cby, sums, hb, db, lefts, rights,
):
    side = Sides(even_in, odd_in, even_out, odd_out)
    lane = side.lane
    second = second_lanes(lane)
    at_h, at_d, at_cx, at_cy, at_g = payload_layout(rows)
    count = rows // 2 + W
    offset = rows // 2 - W
    store = Stores(24)
    for place in range(at_g + 1):
        store(lefts, place, side.left(place))
        right = side.right_divergence(place) if at_d <= place < at_cx else side.right(place)
        store(rights, place, right)
    store.release()

    for ref, target, place in ((cx_ref, cbx, at_cx), (cy_ref, cby, at_cy)):

        def strip_tile(row, shift):
            p, k = divmod(row // 8, GROUPS)
            left = roll(lefts[place + p], 64 - W - W * k + shift)
            right = roll(rights[place + p], shift - W * k)
            return strip(lane, ref[pl.ds(row, 8), :], left, right, shift)

        for row in range(0, count, 8):
            value = jnp.where(second, strip_tile(row + offset, SECOND), strip_tile(row, 0))
            store(target, pl.ds(row, 8), value)

    def strips_at(row, m, k, shift):
        left, right = lefts[at_h + m], rights[at_h + m]
        left, right = roll(left, 64 - W - W * k + shift), roll(right, shift - W * k)
        height = strip(lane, h_ref[row], left, right, shift)
        left, right = lefts[at_d + m], rights[at_d + m]
        left, right = roll(left, 64 - W + 1 - W * k + shift), roll(right, shift - W * k)
        return height, strip_divergence(lane, d_ref[row], left, right, shift)

    def build(b, length):
        for k in range(length):
            row = b * GROUPS + k
            upper = strips_at(row, b, k, 0)
            lower_m, lower_k = divmod(offset + k, GROUPS)
            lower = strips_at(row + offset, b + lower_m, lower_k, SECOND)
            store(bh0, row, jnp.where(second, lower[0], upper[0]))
            store(bd0, row, jnp.where(second, lower[1], upper[1]))

    for b in range(0, count, GROUPS):
        build(b // GROUPS, min(GROUPS, count - b))
    store.release()
    bd0[count] = strip(lane, d_ref[rows], roll(lefts[at_g], 64 - W), rights[at_g])
    first = (bh0, bd0, hb, db, cbx, cby)
    then = (hb, db, hb, db, cbx, cby)
    run_steps(count, range(ITERS), first, then, 24)

    bounds = slot_bounds(rows)
    for u in range(len(bounds) - 1):
        total = jnp.zeros((8, LANES), F32)
        for r in range(max(bounds[u], W), min(bounds[u + 1], rows - W)):
            lower = r >= rows // 2
            value = merge(lane, done_ref[r], hb[r - offset if lower else r], lower)
            store(merged, r, value)
            weight = wet_ref[pl.ds(r, 1), :].astype(F32) * uplift_ref[pl.ds(r, 1), :] * (1.0 / BS)
            total = total + weight * value
        store(sums, u, total)
    store.release()


def slot_bounds(length):
    return [0] + list(range(BS // 2, length, BS)) + [length]


def bands_kernel(
    rows, x_even_in, x_odd_in, h_ref, d_ref, cx_ref, cy_ref, bh0, bd0, cbx, cby, done_wet, uplift_ref, sums_ref, homes_ref,
    edge, message, hs, ds, cxs, cys, cbs,
):
    lane = lanes_of()
    second = second_lanes(lane)
    even = lax.rem(lax.axis_index("gx"), 2) == 0
    depth = 3 * W
    count = rows // 2 + W

    def above(place):
        return jnp.where(even, x_odd_in[place], x_even_in[place])

    def below(place):
        return jnp.where(even, x_even_in[place], x_odd_in[place])

    def both(upper, lower):
        return jnp.where(second, lower, upper)

    store = Stores(24)

    top, bottom, strips = 0, 1, 2
    for c, (ref, mine, packed) in enumerate(((cxs, cx_ref, cbx), (cys, cy_ref, cby))):
        halos = []
        for got, shift in ((above, 0), (below, SECOND)):
            value, corner = got(2 * W + 2 + c), got(2 * W + 4)
            left = roll(corner, 64 - W - 2 * W * c + shift)
            right = roll(corner, shift - W - 2 * W * c)
            halos.append((value, strip(lane, value, left, right, shift)))
        store(ref, (top, slice(0, W)), halos[0][0])
        store(ref, (top, slice(W, depth)), mine[0 : 2 * W, :])
        store(ref, (bottom, slice(0, 2 * W)), mine[rows - 2 * W : rows, :])
        store(ref, (bottom, slice(2 * W, depth)), halos[1][0])
        store(ref, (strips, slice(0, W)), both(halos[0][1], packed[count - 2 * W : count - W, :]))
        store(ref, (strips, slice(W, 2 * W)), both(packed[0:W, :], packed[count - W : count, :]))
        store(
            ref, (strips, slice(2 * W, depth)), both(packed[W : 2 * W, :], halos[1][1])
        )

    def halo_strips(got, j, shift):
        packed_h, packed_d = got(2 * W), got(2 * W + 1)
        left, right = roll(packed_h, 64 - W - W * j + shift), roll(packed_h, shift - 64 - W * j)
        height = strip(lane, got(j), left, right, shift)
        left, right = roll(packed_d, 64 - W + 1 - W * j + shift), roll(packed_d, shift - 64 - W * j)
        return height, strip_divergence(lane, got(W + j), left, right, shift)

    flux, corner = above(2 * W + 5), above(2 * W + 4)
    flux_strip = strip(lane, flux, roll(corner, 64 - W - 4 * W), roll(corner, -5 * W))
    for j in range(W):
        upper, (h_last, d_last) = halo_strips(above, j, 0), halo_strips(below, j, SECOND)
        d_first, d_below = bd0[j], below(W + j)
        d_top = d_ref[j]
        if j == 0:
            d_first = d_first + flux_strip
            d_top = d_top + flux
            d_below = d_below + d_ref[rows]
            d_last = d_last + roll(bd0[count], SECOND)
        low, packed_low = rows - 2 * W + j, count - 2 * W + j
        for band, place, height, divergence in (
            (top, j, above(j), above(W + j)),
            (top, W + j, h_ref[j], d_top),
            (top, 2 * W + j, h_ref[W + j], d_ref[W + j]),
            (bottom, j, h_ref[low], d_ref[low]),
            (bottom, W + j, h_ref[low + W], d_ref[low + W]),
            (bottom, 2 * W + j, below(j), d_below),
            (strips, j, both(upper[0], bh0[packed_low]), both(upper[1], bd0[packed_low])),
            (strips, W + j, both(bh0[j], bh0[packed_low + W]), both(d_first, bd0[packed_low + W])),
            (strips, 2 * W + j, both(bh0[W + j], h_last), both(bd0[W + j], d_last)),
        ):
            store(hs, (band, place), height)
            store(ds, (band, place), divergence)
    store.release()

    for b in range(3):
        for low in range(0, depth, W):
            store(cbs, (b, slice(low, low + W)), roll(cys[b, low : low + W, :], 1))
    store.release()
    views = [(hs.at[b], ds.at[b], hs.at[b], ds.at[b], cxs.at[b], cys.at[b]) for b in range(3)]
    items = []
    for t in range(1, ITERS + 1):
        low, high = t, depth - t
        for b, view in enumerate(views):
            for r in range(low, high):
                items.append(view + (r, r == low, "item" if r + 1 < high else "row", cbs.at[b]))
    advance(items, 8)

    bounds = slot_bounds(rows)
    slots_x = len(bounds) - 1
    totals = [sums_ref[u] for u in range(slots_x)]
    for band, first in ((top, 0), (bottom, rows - W)):
        slot = 0 if band == top else slots_x - 1
        for j in range(W):
            value = merge(lane, hs[band, W + j], hs[strips, W + j], band == bottom)
            store(edge, band * W + j, value)
            weight = done_wet[pl.ds(first + j, 1), :].astype(F32) * uplift_ref[pl.ds(first + j, 1), :] * (1.0 / BS)
            totals[slot] = totals[slot] + weight * value
    store.release()
    column_bounds = slot_bounds(LANES)
    slots_y = len(column_bounds) - 1
    devices = message.shape[0]
    gauge = lax.broadcasted_iota(jnp.int32, (8, LANES), 0)
    shape = (devices, LANES)
    here = lanes_of(shape)
    per_device = 8
    home_of = jnp.where(
        here < per_device * 8,
        lax.broadcasted_iota(jnp.int32, shape, 0) * per_device + here // 8,
        -1,
    )
    built = jnp.zeros(shape, F32)
    for u in range(slots_x):
        for w in range(slots_y):
            inside = (lane >= column_bounds[w]) & (lane < column_bounds[w + 1])
            total = jnp.sum(jnp.where(inside, totals[u], 0.0), axis=1, keepdims=True)
            spread = jnp.sum(jnp.where(lane % 8 == gauge, total, 0.0), axis=0, keepdims=True)
            home = homes_ref[pl.ds(u * slots_y + w, 1), :]
            built = built + jnp.where(home_of == home, spread, 0.0)
    message[...] = built


def write_kernel(rows, merged, edge, out_hbm, sems):
    inner = rows - 2 * W
    copies = []
    for g in range(8):
        for source, at, first, length in (
            (merged, W, W, inner),
            (edge, 0, 0, W),
            (edge, W, rows - W, W),
        ):
            copies.append(
                pltpu.make_async_copy(
                    source.at[pl.ds(at, length), g],
                    out_hbm.at[pl.ds(g * rows + first, length)],
                    sems.at[len(copies)],
                )
            )
    for copy in copies:
        copy.start()
    for copy in copies:
        copy.wait()


def pairs(axis, first):
    return [
        pair
        for i in range(first, lax.axis_size(axis) - 1, 2)
        for pair in ((i, i + 1), (i + 1, i))
    ]


def in_vmem(*arrays):
    return [pltpu.with_memory_space_constraint(array, pltpu.VMEM) for array in arrays]


def in_hbm(array):
    return pltpu.with_memory_space_constraint(array, pltpu.HBM)


def shaped(*shape, dtype=F32):
    return jax.ShapeDtypeStruct(shape, dtype)


def bind(kernel, *sizes):
    def bound(*refs):
        kernel(*sizes, *refs)

    return bound


def body(
    terminal_elevation,
    terminal_flux_x,
    terminal_flux_y,
    courant_x,
    courant_y,
    land_sea,
    uplift,
    tile_patches,
    patch_home,
):
    gauges, rows, columns = terminal_elevation.shape
    flat = (gauges * rows, columns)
    layers = (rows + 8, gauges, columns)
    devices = lax.axis_size("gx") * lax.axis_size("gy")
    slots = tile_patches.shape[2]
    slots_x = len(slot_bounds(rows)) - 1
    vectors = payload_layout(rows)[-1] + 1
    field = pltpu.VMEM((rows, gauges, columns), F32)
    work = pltpu.VMEM(layers, F32)

    height, divergence, odd_out, even_out, courant_x, courant_y, homes = pl.pallas_call(
        bind(load_kernel, rows),
        out_shape=(
            shaped(*layers), shaped(*layers), shaped(vectors, 8, columns), shaped(vectors, 8, columns),
            shaped(rows, columns), shaped(rows, columns), shaped(slots, columns, dtype=jnp.int32),
        ),
        in_specs=[HBM] * 8,
        out_specs=(VMEM,) * 7,
        scratch_shapes=[field] * 3
        + [
            pltpu.VMEM((rows, columns), jnp.int32),
            pltpu.SMEM(tile_patches.shape, jnp.int32),
            pltpu.SMEM(patch_home.shape, jnp.int32),
            pltpu.SemaphoreType.DMA((11,)),
        ],
        compiler_params=params(LOAD_MIB),
        name="load",
    )(
        in_hbm(terminal_elevation.reshape(flat)),
        in_hbm(terminal_flux_x.reshape(flat)),
        in_hbm(terminal_flux_y.reshape(flat)),
        in_hbm(courant_x),
        in_hbm(courant_y),
        in_hbm(land_sea),
        in_hbm(tile_patches),
        in_hbm(patch_home),
    )
    odd_in = lax.ppermute(odd_out, "gy", pairs("gy", 1))
    even_in = lax.ppermute(even_out, "gy", pairs("gy", 0))

    center_h, center_d, token = pl.pallas_call(
        bind(center_first_kernel, rows, range(EARLY)),
        out_shape=(shaped(*layers), shaped(*layers), shaped(8, columns)),
        in_specs=[VMEM] * 4,
        out_specs=(VMEM,) * 3,
        compiler_params=params(2),
        cost_estimate=pl.CostEstimate(flops=COST, bytes_accessed=2**20, transcendentals=0),
        name="center_first",
    )(*in_vmem(height, divergence, courant_x, courant_y))

    x_even_out, x_odd_out = pl.pallas_call(
        bind(middle_kernel, rows),
        out_shape=(shaped(MESSAGE, 8, columns),) * 2,
        in_specs=[VMEM] * 9,
        out_specs=(VMEM,) * 2,
        compiler_params=params(2),
        name="middle",
    )(*in_vmem(even_in, odd_in, even_out, odd_out, height, divergence, courant_x, courant_y, token))
    x_even_in = lax.ppermute(x_even_out, "gx", pairs("gx", 0))
    x_odd_in = lax.ppermute(x_odd_out, "gx", pairs("gx", 1))

    center, _ = pl.pallas_call(
        bind(center_second_kernel, rows, range(EARLY, ITERS)),
        out_shape=(shaped(*layers),) * 2,
        in_specs=[VMEM] * 4,
        out_specs=(VMEM,) * 2,
        input_output_aliases={0: 0, 1: 1},
        compiler_params=params(2),
        cost_estimate=pl.CostEstimate(flops=COST, bytes_accessed=2**20, transcendentals=0),
        name="center_second",
    )(*in_vmem(center_h, center_d, courant_x, courant_y))

    count = rows // 2 + W
    packed = (count + 8, gauges, columns)
    merged, bh0, bd0, cbx, cby, sums = pl.pallas_call(
        bind(strips_kernel, rows),
        out_shape=(
            shaped(rows, gauges, columns), shaped(*packed), shaped(*packed), shaped(count, columns), shaped(count, columns),
            shaped(slots_x, 8, columns),
        ),
        in_specs=[VMEM] * 11,
        out_specs=(VMEM,) * 6,
        scratch_shapes=[pltpu.VMEM(packed, F32)] * 2 + [pltpu.VMEM((vectors, 8, columns), F32)] * 2,
        compiler_params=params(5),
        cost_estimate=pl.CostEstimate(flops=COST, bytes_accessed=2**20, transcendentals=0),
        name="strips",
    )(
        *in_vmem(even_in, odd_in, even_out, odd_out, height, divergence, courant_x, courant_y, center),
        land_sea, uplift,
    )

    depth = 3 * W
    edge, message = pl.pallas_call(
        bind(bands_kernel, rows),
        out_shape=(shaped(2 * W, gauges, columns), shaped(devices, columns)),
        in_specs=[VMEM] * 14,
        out_specs=(VMEM,) * 2,
        scratch_shapes=[
            pltpu.VMEM((3, depth, 8, columns), F32),
            pltpu.VMEM((3, depth, 8, columns), F32),
            pltpu.VMEM((3, depth, columns), F32),
            pltpu.VMEM((3, depth, columns), F32),
            pltpu.VMEM((3, depth, columns), F32),
        ],
        compiler_params=params(2),
        name="bands",
    )(
        *in_vmem(x_even_in, x_odd_in, height, divergence, courant_x, courant_y, bh0, bd0, cbx, cby),
        land_sea, uplift, *in_vmem(sums, homes),
    )
    received = lax.all_to_all(message, ("gx", "gy"), 0, 0, tiled=True)
    out = pl.pallas_call(
        bind(write_kernel, rows),
        out_shape=shaped(*flat),
        in_specs=[VMEM] * 2,
        out_specs=HBM,
        scratch_shapes=[pltpu.SemaphoreType.DMA((24,))],
        compiler_params=params(1),
        name="write",
    )(*in_vmem(merged, edge))
    per_device = patch_home.shape[0] // devices
    gradient = jnp.sum(received, axis=0)[: per_device * gauges].reshape(per_device, gauges)
    return (out.reshape(gauges, rows, columns), gradient)


LOAD_MIB = 6
COST = 40_000_000
EARLY = 6


def solution(mesh):
    in_specs = (
        P(None, "gx", "gy"),
        P(None, "gx", "gy"),
        P(None, "gx", "gy"),
        P("gx", "gy"),
        P("gx", "gy"),
        P("gx", "gy"),
        P("gx", "gy"),
        P(),
        P(),
    )
    out_specs = (P(None, "gx", "gy"), P(("gx", "gy"), None))
    return jax.shard_map(body, mesh=mesh, in_specs=in_specs, out_specs=out_specs, check_vma=False)
```
